32 devices in a mesh: groups: 2 (over x), adapter: 16 (over z, y, core).
Axes of the slice: x: 2, y: 2, z: 4, core: 2. Of those that a mesh axis runs over, the one named last changes fastest.
Arguments:
- activations: bfloat16 [4096, 8192], P(('groups', 'adapter')), parts along dimension 0, may hold values from -6 to 6
- cotangent: bfloat16 [4096, 1024], P(('groups', 'adapter')), parts along dimension 0, may hold values from -1.5 to 1.5
- family: int32 [4096], P(('groups', 'adapter')), parts along dimension 0, may hold values from 0 to 127, as said below
- value_weight: bfloat16 [8192, 1024], P('adapter'), may hold values from -0.1875 to 0.1875
- adapter_down: bfloat16 [8192, 8192], P(None, 'adapter'), may hold values from -0.0625 to 0.0625
- adapter_up: bfloat16 [8192, 1024], P('adapter'), may hold values from -0.1875 to 0.1875
Outputs:
- input_gradient: bfloat16 [4096, 8192], P(('groups', 'adapter')), parts along dimension 0
- grad_down: bfloat16 [16384, 8192], P('groups', 'adapter'), parts along dimension 0
- grad_up: bfloat16 [8192, 2048], P('adapter', 'groups'), parts along dimension 1
The draws below stay inside these ranges and needn't reach their ends.
There are 2 independent parts, one for each index of `groups`. The reference program is written for one: setup_inputs(seed, part) draws one part's arguments, and reference() takes and returns one part's arrays. A program takes and returns all parts, laid end to end along the dimension named above; an argument that names none is the same for every part. Nothing has to cross between parts.
Inputs may be any that keep to these rules, and one draw needn't show every extreme that they name: Family f is owned by index f // 8 of adapter. Among the 128 tokens of one index of adapter, those whose families one index owns all have the same family, and there are at most 16 of them; in every draw one owner receives exactly 16 tokens from every index of adapter.
All inputs are finite; a program needn't handle non-finite values.
Results may differ from the reference program's by a relative error of at most 0.0085.
Values may be sent and summed in bfloat16 or wider, within the bound.
No kernel may reach another device: no remote copies, remote signals or barrier semaphores. Data moves between devices by JAX's collectives and lax.ppermute only.
A program may use at most 128 MiB of HBM per device.

```python
import math
import jax
import jax.numpy as jnp
from jax import lax

MODEL_WIDTH = 8192
VALUE_FEATURES = 1024
ADAPTER_RANK = 64
FAM_DEV = 8
TOK_DEV = 128
FAMILY_COUNT = 128
TOKENS = 2048
TOKEN_LIMIT = 16
N_ADAPTER = 16


def draw_family(key, part):
    key = jax.random.fold_in(key, 11)
    key_hot, key_noise, key_pick, key_order = jax.random.split(key, 4)
    token_slots = N_ADAPTER * TOKEN_LIMIT
    popular_family = jax.random.randint(key_hot, (), 0, N_ADAPTER)
    random_jitter = jax.random.randint(key_noise, (N_ADAPTER, token_slots), 0, 1 << 20)
    family_index = jnp.arange(token_slots, dtype=jnp.int32)
    extra_score = jnp.where(family_index // TOKEN_LIMIT == popular_family, 1 << 30, 0).astype(jnp.int32)
    family_scores = random_jitter * token_slots + family_index[None, :] + extra_score[None, :]
    values, chosen = lax.top_k(family_scores, TOK_DEV)
    owner = (chosen // TOKEN_LIMIT).astype(jnp.int32)
    picks = jax.random.randint(key_pick, (N_ADAPTER, N_ADAPTER), 0, FAM_DEV)
    fam = owner * FAM_DEV + jnp.take_along_axis(picks, owner, axis=1)
    shuffle = jax.random.randint(key_order, (N_ADAPTER, TOK_DEV), 0, 1 << 20) * TOK_DEV + jnp.arange(TOK_DEV, dtype=jnp.int32)[None, :]
    order = jnp.argsort(shuffle, axis=1)
    fam = jnp.take_along_axis(fam, order, axis=1)
    return fam.reshape(-1).astype(jnp.int32)


def block_scale(key, extent, cuts, low, largest):
    gain = 1.0
    for axis_at, shards_of in cuts:
        steps = jax.random.uniform(jax.random.fold_in(jax.random.fold_in(key, 6), axis_at), (shards_of,), jnp.float32, low / len(cuts), largest / len(cuts))
        gain = gain * jnp.repeat(jnp.exp(steps), extent[axis_at] // shards_of).reshape((-1,) + (1,) * (len(extent) - 1 - axis_at))
    return gain


def bell_draw(own_key, shape, scale, most, cuts=(), kind=jnp.bfloat16):
    gain = block_scale(own_key, shape, cuts, -0.22, 0.18) if cuts else 1.0
    values = jax.random.normal(own_key, shape, jnp.float32) * scale * gain
    return jnp.minimum(jnp.maximum(values, -most), most).astype(kind)


def setup_inputs(seed: int = 0, part: int = 0) -> dict:
    key_list = jax.random.split(jax.random.key(seed), 7)
    part_keys = jax.random.split(jax.random.fold_in(key_list[6], part), 7)
    return {
        "activations": bell_draw(part_keys[0], (TOKENS, MODEL_WIDTH), 1.0, 6.0, ((0, 16),)),
        "cotangent": bell_draw(part_keys[1], (TOKENS, VALUE_FEATURES), 0.25, 1.5, ((0, 16),)),
        "family": draw_family(jax.random.fold_in(jax.random.fold_in(key_list[6], part), 71), part),
        "value_weight": bell_draw(key_list[3], (MODEL_WIDTH, VALUE_FEATURES), VALUE_FEATURES ** -0.5, 0.1875, ((0, 16),)),
        "adapter_down": bell_draw(key_list[4], (MODEL_WIDTH, FAMILY_COUNT * ADAPTER_RANK), MODEL_WIDTH ** -0.5, 0.0625, ((1, 16),)),
        "adapter_up": bell_draw(key_list[5], (FAMILY_COUNT * ADAPTER_RANK, VALUE_FEATURES), VALUE_FEATURES ** -0.5, 0.1875, ((0, 16),)),
    }


SCALE = 2.0


def reference(activations, cotangent, family, value_weight, adapter_down, adapter_up):
    frozen_part = jnp.dot(cotangent, value_weight.T, preferred_element_type=jnp.float32).astype(jnp.bfloat16)
    down_blocks3 = adapter_down.reshape(MODEL_WIDTH, FAMILY_COUNT, ADAPTER_RANK)
    up_blocks3 = adapter_up.reshape(FAMILY_COUNT, ADAPTER_RANK, VALUE_FEATURES)
    width = math.gcd(TOKENS, 128)
    x_blocks = activations.reshape(-1, width, MODEL_WIDTH)
    g_blocks = cotangent.reshape(-1, width, VALUE_FEATURES)
    f_blocks = family.reshape(-1, width)

    def step(carry, items):
        acc_down, acc_up = carry
        xb, gb, fb = items
        a_tok = jnp.take(down_blocks3, fb, axis=1).astype(jnp.float32)
        b_tok = jnp.take(up_blocks3, fb, axis=0).astype(jnp.float32)
        xf = xb.astype(jnp.float32)
        gf = gb.astype(jnp.float32)
        low_rank_product = jnp.einsum('td,dtr->tr', xf, a_tok).astype(jnp.bfloat16)
        backward_rows = jnp.einsum('tk,trk->tr', gf, b_tok).astype(jnp.bfloat16)
        backf = backward_rows.astype(jnp.float32)
        rows = (SCALE * jnp.einsum('tr,dtr->td', backf, a_tok)).astype(jnp.bfloat16)
        acc_down = acc_down.at[:, fb, :].add(jnp.einsum('td,tr->dtr', xf, backf))
        acc_up = acc_up.at[fb].add(jnp.einsum('tr,tk->trk', low_rank_product.astype(jnp.float32), gf))
        return (acc_down, acc_up), rows

    init = (jnp.zeros((MODEL_WIDTH, FAMILY_COUNT, ADAPTER_RANK), jnp.float32), jnp.zeros((FAMILY_COUNT, ADAPTER_RANK, VALUE_FEATURES), jnp.float32))
    (acc_down, acc_up), rows = lax.scan(step, init, (x_blocks, g_blocks, f_blocks))
    rows = rows.reshape(TOKENS, MODEL_WIDTH)
    input_gradient = (frozen_part.astype(jnp.float32) + rows.astype(jnp.float32)).astype(jnp.bfloat16)
    grad_down = (SCALE * acc_down).reshape(MODEL_WIDTH, FAMILY_COUNT * ADAPTER_RANK).astype(jnp.bfloat16)
    grad_up = (SCALE * acc_up).reshape(FAMILY_COUNT * ADAPTER_RANK, VALUE_FEATURES).astype(jnp.bfloat16)
    return (input_gradient, grad_down, grad_up)
```

```python
import functools

import jax
import jax.numpy as jnp
from jax import lax
from jax.experimental import pallas as pl
from jax.experimental.pallas import tpu as pltpu
from jax.sharding import PartitionSpec as P

ADAPTER_RANK = 64
FAM_DEV = 8
PLANE = 8
LANES = 128
BLOCK = 1024
VMEM = 60 << 20


SCALE = 2.0


def dot(a, b, dims):
    return lax.dot_general(a, b, (dims, ((), ())), preferred_element_type=jnp.float32)


def pack_kernel(cap, family_ref, dy_ref, out_ref, place_ref, back_place_ref):
    tok_rows, features = dy_ref.shape
    token_slots = out_ref.shape[0]
    square = (tok_rows, tok_rows)
    along = jnp.broadcast_to(family_ref[...], square)
    down = along.T
    same = (along // FAM_DEV) == (down // FAM_DEV)
    row = lax.broadcasted_iota(jnp.int32, square, 0)
    column = lax.broadcasted_iota(jnp.int32, square, 1)
    rank_down = jnp.sum((same & (column < row)).astype(jnp.int32), axis=1, keepdims=True)
    rank_along = jnp.sum((same & (row < column)).astype(jnp.int32), axis=0, keepdims=True)
    slot_down = (down[:, :1] // FAM_DEV) * cap + rank_down
    slot_along = (along[:1] // FAM_DEV) * cap + rank_along
    slots = lax.broadcasted_iota(jnp.int32, (token_slots, tok_rows), 0)
    place = jnp.where(slots == slot_along, 1.0, 0.0).astype(jnp.bfloat16)
    place_ref[...] = place
    slots = lax.broadcasted_iota(jnp.int32, (tok_rows, token_slots), 1)
    back_place_ref[...] = jnp.where(slots == slot_down, 1.0, 0.0).astype(jnp.bfloat16)
    out_ref[:, :features] = dot(place, dy_ref[...], ((1,), (0,))).astype(jnp.bfloat16)
    families = (down % FAM_DEV).astype(jnp.float32)[:, :LANES].astype(jnp.bfloat16)
    out_ref[:, features:] = dot(place, families, ((1,), (0,))).astype(jnp.bfloat16)


def pack(family, cotangent, cap, token_slots):
    tok_rows, features = cotangent.shape
    return pl.pallas_call(
        functools.partial(pack_kernel, cap),
        out_shape=[
            jax.ShapeDtypeStruct((token_slots, features + LANES), jnp.bfloat16),
            jax.ShapeDtypeStruct((token_slots, tok_rows), jnp.bfloat16),
            jax.ShapeDtypeStruct((tok_rows, token_slots), jnp.bfloat16),
        ],
        compiler_params=pltpu.CompilerParams(vmem_limit_bytes=VMEM),
    )(family.reshape(1, tok_rows), cotangent)


def own_columns(family_ref, columns):
    shape = (family_ref.shape[0], columns)
    column_family = lax.broadcasted_iota(jnp.int32, shape, 1) // ADAPTER_RANK
    return column_family == family_ref[:, :1].astype(jnp.int32)


def rows_kernel(dy_ref, family_ref, up_ref, down_ref, rows_ref, backward_ref):
    @pl.when(pl.program_id(0) == 0)
    def _():
        back = dot(dy_ref[...], up_ref[...], ((1,), (1,)))
        keep = own_columns(family_ref, back.shape[1])
        backward_ref[...] = jnp.where(keep, back, 0.0).astype(jnp.bfloat16)

    rows = dot(backward_ref[...], down_ref[...], ((1,), (1,)))
    rows_ref[...] = (SCALE * rows).astype(jnp.bfloat16)


def make_rows(received, adapter_up, adapter_down):
    token_slots = received.shape[0]
    columns, features = adapter_up.shape
    width = adapter_down.shape[0]
    return pl.pallas_call(
        rows_kernel,
        grid=(width // BLOCK,),
        in_specs=[
            pl.BlockSpec((token_slots, features), lambda j: (0, 0)),
            pl.BlockSpec((token_slots, LANES), lambda j: (0, features // LANES)),
            pl.BlockSpec((columns, features), lambda j: (0, 0)),
            pl.BlockSpec((BLOCK, columns), lambda j: (j, 0)),
        ],
        out_specs=[
            pl.BlockSpec((token_slots, BLOCK), lambda j: (0, j)),
            pl.BlockSpec((token_slots, columns), lambda j: (0, 0)),
        ],
        out_shape=[
            jax.ShapeDtypeStruct((token_slots, width), jnp.bfloat16),
            jax.ShapeDtypeStruct((token_slots, columns), jnp.bfloat16),
        ],
        compiler_params=pltpu.CompilerParams(vmem_limit_bytes=VMEM),
        cost_estimate=pl.CostEstimate(
            flops=2 * token_slots * columns * (width + features),
            bytes_accessed=2 * (columns + token_slots) * (width + features),
            transcendentals=0,
        ),
    )(received, received, adapter_up, adapter_down)


def grads_kernel(x_ref, dy_ref, family_ref, backward_ref, down_ref, grad_down_ref, grad_up_ref, low_ref):
    step = pl.program_id(0)

    @pl.when(step == 0)
    def _():
        low_ref[...] = jnp.zeros_like(low_ref)

    low_ref[...] += dot(x_ref[...], down_ref[...], ((1,), (0,)))
    grad_down = dot(x_ref[...], backward_ref[...], ((0,), (0,)))
    grad_down_ref[...] = (SCALE * grad_down).astype(jnp.bfloat16)

    @pl.when(step == pl.num_programs(0) - 1)
    def _():
        keep = own_columns(family_ref, low_ref.shape[1])
        low = jnp.where(keep, low_ref[...], 0.0).astype(jnp.bfloat16)
        grad_up = dot(low, dy_ref[...], ((0,), (0,)))
        grad_up_ref[...] = (SCALE * grad_up).astype(jnp.bfloat16)


def make_grads(received_input, received, backward_rows, adapter_up, adapter_down):
    token_slots = received.shape[0]
    columns, features = adapter_up.shape
    width = adapter_down.shape[0]
    return pl.pallas_call(
        grads_kernel,
        grid=(width // BLOCK,),
        in_specs=[
            pl.BlockSpec((token_slots, BLOCK), lambda j: (0, j)),
            pl.BlockSpec((token_slots, features), lambda j: (0, 0)),
            pl.BlockSpec((token_slots, LANES), lambda j: (0, features // LANES)),
            pl.BlockSpec((token_slots, columns), lambda j: (0, 0)),
            pl.BlockSpec((BLOCK, columns), lambda j: (j, 0)),
        ],
        out_specs=[
            pl.BlockSpec((BLOCK, columns), lambda j: (j, 0)),
            pl.BlockSpec((columns, features), lambda j: (0, 0)),
        ],
        out_shape=[
            jax.ShapeDtypeStruct((width, columns), jnp.bfloat16),
            jax.ShapeDtypeStruct((columns, features), jnp.bfloat16),
        ],
        scratch_shapes=[pltpu.VMEM((token_slots, columns), jnp.float32)],
        compiler_params=pltpu.CompilerParams(vmem_limit_bytes=VMEM),
        cost_estimate=pl.CostEstimate(
            flops=2 * token_slots * columns * (2 * width + features),
            bytes_accessed=2 * (2 * columns + token_slots) * (width + features),
            transcendentals=0,
        ),
    )(received_input, received, received, backward_rows, adapter_down)


def finish_kernel(share, groups, at_ref, place_ref, rows_ref, base_ref, out_ref):
    inner = PLANE // groups
    for layer in range(base_ref.shape[2] // share):
        for block in range(PLANE):
            start = (layer * PLANE + block) * share
            columns = slice(start, start + share)
            adapter_part = dot(place_ref[...], rows_ref[:, columns], ((1,), (0,)))
            inner_shift = lax.rem(at_ref[0] - block // groups + inner, inner)
            group_shift = lax.rem(at_ref[1] - block % groups + groups, groups)
            base = base_ref[inner_shift * groups + group_shift]
            base = base[:, layer * share : (layer + 1) * share].astype(jnp.float32)
            out_ref[:, columns] = (base + adapter_part).astype(jnp.bfloat16)


def finish(at, place, rows, base, deep, groups):
    tok_rows, token_slots = place.shape
    width = rows.shape[1]
    share = base.shape[2] // deep
    layers = max(1, LANES // share)
    steps = deep // layers
    return pl.pallas_call(
        functools.partial(finish_kernel, share, groups),
        grid_spec=pltpu.PrefetchScalarGridSpec(
            num_scalar_prefetch=1,
            grid=(steps,),
            in_specs=[
                pl.BlockSpec((tok_rows, token_slots), lambda z, _: (0, 0)),
                pl.BlockSpec((token_slots, width // steps), lambda z, _: (0, z)),
                pl.BlockSpec((PLANE, tok_rows, share * layers), lambda z, _: (0, 0, z)),
            ],
            out_specs=pl.BlockSpec((tok_rows, width // steps), lambda z, _: (0, z)),
        ),
        out_shape=jax.ShapeDtypeStruct((tok_rows, width), jnp.bfloat16),
        compiler_params=pltpu.CompilerParams(vmem_limit_bytes=VMEM),
        cost_estimate=pl.CostEstimate(
            flops=2 * tok_rows * token_slots * width,
            bytes_accessed=2 * width * (token_slots + 2 * tok_rows),
            transcendentals=0,
        ),
    )(at, place, rows, base)


def local(activations, cotangent, family, value_weight, adapter_down, adapter_up):
    count = lax.axis_size("adapter")
    groups = lax.axis_size("groups")
    inner = PLANE // groups
    deep = count // inner
    tok_rows, width = activations.shape
    cap = max(2, (2 * tok_rows + count - 1) // count)
    token_slots = count * cap
    me = lax.axis_index("adapter")
    my_group = lax.axis_index("groups")
    my_inner = lax.rem(me, inner)
    my_layer = me // inner

    def around_groups(block, shift):
        pairs = [(j, (j + shift) % groups) for j in range(groups)]
        return lax.ppermute(block, "groups", pairs)

    def around_plane(block, shift):
        pairs = [
            (line * inner + j, line * inner + (j + shift) % inner)
            for line in range(deep)
            for j in range(inner)
        ]
        return lax.ppermute(block, "adapter", pairs)

    def next_layer(block, step):
        pairs = [(j, j + step) for j in range(count) if 0 <= j + step < count]
        return lax.ppermute(block, "adapter", pairs)

    send, place, back_place = pack(family, cotangent, cap, token_slots)
    received = lax.all_to_all(send, "adapter", split_axis=0, concat_axis=0, tiled=True)

    share = value_weight.shape[0] // groups
    own_share = lax.dynamic_slice_in_dim(value_weight, my_group * share, share, 0)
    layers = [own_share]
    up = down = own_share
    for _ in range(deep - 1):
        up, down = next_layer(up, inner), next_layer(down, -inner)
        layers = [up] + layers + [down]

    send_x = dot(place, activations, ((1,), (0,))).astype(jnp.bfloat16)
    send_x, layers, cotangent = lax.optimization_barrier((send_x, layers, cotangent))
    received_input = lax.all_to_all(send_x, "adapter", split_axis=0, concat_axis=0, tiled=True)

    plane_weight = lax.dynamic_slice_in_dim(
        jnp.concatenate(layers, axis=0), (deep - 1 - my_layer) * share, deep * share, 0
    )
    plane_dy = [cotangent] + [around_groups(cotangent, -shift) for shift in range(1, groups)]
    plane_dy = jnp.stack(plane_dy)
    plane_dy = [plane_dy] + [around_plane(plane_dy, -shift) for shift in range(1, inner)]
    plane_dy = [jnp.concatenate([d[s] for d in plane_dy], axis=0) for s in range(groups)]

    adapter_rows, backward_rows = make_rows(received, adapter_up, adapter_down)
    blocks = [dot(block, plane_weight, ((1,), (1,))).astype(jnp.bfloat16) for block in plane_dy]
    blocks = blocks[:1] + [around_groups(block, s) for s, block in enumerate(blocks) if s]
    adapter_rows, received_input, blocks = lax.optimization_barrier(
        (adapter_rows, received_input, blocks)
    )
    returned_rows = lax.all_to_all(adapter_rows, "adapter", split_axis=0, concat_axis=0, tiled=True)
    base = []
    for shift in range(inner):
        for block in blocks:
            piece = block[shift * tok_rows : (shift + 1) * tok_rows]
            base.append(around_plane(piece, shift) if shift else piece)
    base = jnp.stack(base)
    grad_down, grad_up = make_grads(
        received_input, received, backward_rows, adapter_up, adapter_down
    )
    at = jnp.stack([my_inner, my_group]).astype(jnp.int32)
    input_gradient = finish(at, back_place, returned_rows, base, deep, groups)
    return (input_gradient, grad_down, grad_up)


def solution(mesh):
    in_specs = (
        P(("groups", "adapter"), None),
        P(("groups", "adapter"), None),
        P(("groups", "adapter")),
        P("adapter", None),
        P(None, "adapter"),
        P("adapter", None),
    )
    out_specs = (P(("groups", "adapter"), None), P("groups", "adapter"), P("adapter", "groups"))
    return jax.shard_map(local, mesh=mesh, in_specs=in_specs, out_specs=out_specs, check_vma=False)
```

```python
import functools

import jax
import jax.numpy as jnp
from jax import lax
from jax.experimental import pallas as pl
from jax.experimental.pallas import tpu as pltpu
from jax.sharding import PartitionSpec as P

ADAPTER_RANK = 64
FAM_DEV = 8
PLANE = 8
LANES = 128
BLOCK = 1024
VMEM = 60 << 20


SCALE = 2.0


def dot(a, b, dims):
    return lax.dot_general(a, b, (dims, ((), ())), preferred_element_type=jnp.float32)


def pack_kernel(cap, family_ref, dy_ref, out_ref, place_ref, back_place_ref):
    tok_rows, features = dy_ref.shape
    token_slots = out_ref.shape[0]
    square = (tok_rows, tok_rows)
    along = jnp.broadcast_to(family_ref[...], square)
    down = along.T
    same = (along // FAM_DEV) == (down // FAM_DEV)
    row = lax.broadcasted_iota(jnp.int32, square, 0)
    column = lax.broadcasted_iota(jnp.int32, square, 1)
    rank_down = jnp.sum((same & (column < row)).astype(jnp.int32), axis=1, keepdims=True)
    rank_along = jnp.sum((same & (row < column)).astype(jnp.int32), axis=0, keepdims=True)
    slot_down = (down[:, :1] // FAM_DEV) * cap + rank_down
    slot_along = (along[:1] // FAM_DEV) * cap + rank_along
    slots = lax.broadcasted_iota(jnp.int32, (token_slots, tok_rows), 0)
    place = jnp.where(slots == slot_along, 1.0, 0.0).astype(jnp.bfloat16)
    place_ref[...] = place
    slots = lax.broadcasted_iota(jnp.int32, (tok_rows, token_slots), 1)
    back_place_ref[...] = jnp.where(slots == slot_down, 1.0, 0.0).astype(jnp.bfloat16)
    out_ref[:, :features] = dot(place, dy_ref[...], ((1,), (0,))).astype(jnp.bfloat16)
    families = (down % FAM_DEV).astype(jnp.float32)[:, :LANES].astype(jnp.bfloat16)
    out_ref[:, features:] = dot(place, families, ((1,), (0,))).astype(jnp.bfloat16)


def pack(family, cotangent, cap, token_slots):
    tok_rows, features = cotangent.shape
    return pl.pallas_call(
        functools.partial(pack_kernel, cap),
        out_shape=[
            jax.ShapeDtypeStruct((token_slots, features + LANES), jnp.bfloat16),
            jax.ShapeDtypeStruct((token_slots, tok_rows), jnp.bfloat16),
            jax.ShapeDtypeStruct((tok_rows, token_slots), jnp.bfloat16),
        ],
        compiler_params=pltpu.CompilerParams(vmem_limit_bytes=VMEM),
    )(family.reshape(1, tok_rows), cotangent)


def own_columns(family_ref, columns):
    shape = (family_ref.shape[0], columns)
    column_family = lax.broadcasted_iota(jnp.int32, shape, 1) // ADAPTER_RANK
    return column_family == family_ref[:, :1].astype(jnp.int32)


def rows_kernel(
    received_ref, up_ref, down_ref, rows_ref, backward_ref, dy, families, up, down, rows, sems
):
    width, columns = down.shape
    features = dy.shape[1]
    steps = width // BLOCK
    first = [
        pltpu.make_async_copy(received_ref.at[:, pl.ds(0, features)], dy, sems.at[0]),
        pltpu.make_async_copy(up_ref, up, sems.at[1]),
        pltpu.make_async_copy(
            received_ref.at[:, pl.ds(features, LANES)], families, sems.at[2]
        ),
    ]
    loads, stores = [], []
    for step in range(steps):
        part = pl.ds(step * BLOCK, BLOCK)
        loads.append(pltpu.make_async_copy(down_ref.at[part], down.at[part], sems.at[3 + step]))
        stores.append(
            pltpu.make_async_copy(
                rows.at[:, part], rows_ref.at[:, part], sems.at[3 + steps + step]
            )
        )
    for copy in first + loads:
        copy.start()
    for copy in first:
        copy.wait()
    back = dot(dy[...], up[...], ((1,), (1,)))
    back = jnp.where(own_columns(families, columns), back, 0.0).astype(jnp.bfloat16)
    backward_ref[...] = back
    for step in range(steps):
        part = pl.ds(step * BLOCK, BLOCK)
        loads[step].wait()
        product = dot(back, down[part], ((1,), (1,)))
        rows[:, part] = (SCALE * product).astype(jnp.bfloat16)
        stores[step].start()
    for copy in stores:
        copy.wait()


def make_rows(received, adapter_up, adapter_down):
    token_slots = received.shape[0]
    columns, features = adapter_up.shape
    width = adapter_down.shape[0]
    return pl.pallas_call(
        rows_kernel,
        in_specs=[pl.BlockSpec(memory_space=pl.ANY)] * 3,
        out_specs=[
            pl.BlockSpec(memory_space=pl.ANY),
            pl.BlockSpec(memory_space=pltpu.VMEM),
        ],
        out_shape=[
            jax.ShapeDtypeStruct((token_slots, width), jnp.bfloat16),
            jax.ShapeDtypeStruct((token_slots, columns), jnp.bfloat16),
        ],
        scratch_shapes=[
            pltpu.VMEM((token_slots, features), jnp.bfloat16),
            pltpu.VMEM((token_slots, LANES), jnp.bfloat16),
            pltpu.VMEM((columns, features), jnp.bfloat16),
            pltpu.VMEM((width, columns), jnp.bfloat16),
            pltpu.VMEM((token_slots, width), jnp.bfloat16),
            pltpu.SemaphoreType.DMA((3 + 2 * (width // BLOCK),)),
        ],
        compiler_params=pltpu.CompilerParams(vmem_limit_bytes=VMEM),
        cost_estimate=pl.CostEstimate(
            flops=2 * token_slots * columns * (width + features),
            bytes_accessed=2 * (columns + token_slots) * (width + features),
            transcendentals=0,
        ),
    )(received, adapter_up, adapter_down)


def grads_kernel(x_ref, dy_ref, family_ref, backward_ref, down_ref, grad_down_ref, grad_up_ref, low_ref):
    step = pl.program_id(0)

    @pl.when(step == 0)
    def _():
        low_ref[...] = jnp.zeros_like(low_ref)

    low_ref[...] += dot(x_ref[...], down_ref[...], ((1,), (0,)))
    grad_down = dot(x_ref[...], backward_ref[...], ((0,), (0,)))
    grad_down_ref[...] = (SCALE * grad_down).astype(jnp.bfloat16)

    @pl.when(step == pl.num_programs(0) - 1)
    def _():
        keep = own_columns(family_ref, low_ref.shape[1])
        low = jnp.where(keep, low_ref[...], 0.0).astype(jnp.bfloat16)
        grad_up = dot(low, dy_ref[...], ((0,), (0,)))
        grad_up_ref[...] = (SCALE * grad_up).astype(jnp.bfloat16)


def make_grads(received_input, received, backward_rows, adapter_up, adapter_down):
    token_slots = received.shape[0]
    columns, features = adapter_up.shape
    width = adapter_down.shape[0]
    return pl.pallas_call(
        grads_kernel,
        grid=(width // BLOCK,),
        in_specs=[
            pl.BlockSpec((token_slots, BLOCK), lambda j: (0, j)),
            pl.BlockSpec((token_slots, features), lambda j: (0, 0)),
            pl.BlockSpec((token_slots, LANES), lambda j: (0, features // LANES)),
            pl.BlockSpec((token_slots, columns), lambda j: (0, 0)),
            pl.BlockSpec((BLOCK, columns), lambda j: (j, 0)),
        ],
        out_specs=[
            pl.BlockSpec((BLOCK, columns), lambda j: (j, 0)),
            pl.BlockSpec((columns, features), lambda j: (0, 0)),
        ],
        out_shape=[
            jax.ShapeDtypeStruct((width, columns), jnp.bfloat16),
            jax.ShapeDtypeStruct((columns, features), jnp.bfloat16),
        ],
        scratch_shapes=[pltpu.VMEM((token_slots, columns), jnp.float32)],
        compiler_params=pltpu.CompilerParams(vmem_limit_bytes=VMEM),
        cost_estimate=pl.CostEstimate(
            flops=2 * token_slots * columns * (2 * width + features),
            bytes_accessed=2 * (2 * columns + token_slots) * (width + features),
            transcendentals=0,
        ),
    )(received_input, received, received, backward_rows, adapter_down)


def finish_kernel(
    share, groups, at_ref, place_ref, rows_ref, base_ref, out_ref, rows, base, out, sems
):
    inner = PLANE // groups
    wide = PLANE * share
    layers = max(1, LANES // share)
    steps = base.shape[2] // (layers * share)
    loads, stores = [], []
    for step in range(steps):
        part = pl.ds(step * layers * wide, layers * wide)
        side = pl.ds(step * layers * share, layers * share)
        loads.append(
            (
                pltpu.make_async_copy(base_ref.at[:, :, side], base.at[:, :, side], sems.at[step]),
                pltpu.make_async_copy(
                    rows_ref.at[:, part], rows.at[:, part], sems.at[steps + step]
                ),
            )
        )
        stores.append(
            pltpu.make_async_copy(
                out.at[:, part], out_ref.at[:, part], sems.at[2 * steps + step]
            )
        )
    for pair in loads:
        for copy in pair:
            copy.start()
    for step in range(steps):
        for copy in loads[step]:
            copy.wait()
        for layer in range(step * layers, (step + 1) * layers):
            for block in range(PLANE):
                columns = pl.ds((layer * PLANE + block) * share, share)
                adapter_part = dot(place_ref[...], rows[:, columns], ((1,), (0,)))
                inner_shift = lax.rem(at_ref[0] - block // groups + inner, inner)
                group_shift = lax.rem(at_ref[1] - block % groups + groups, groups)
                frozen_part = base[inner_shift * groups + group_shift]
                frozen_part = frozen_part[:, layer * share : (layer + 1) * share]
                total = frozen_part.astype(jnp.float32) + adapter_part
                out[:, columns] = total.astype(jnp.bfloat16)
        stores[step].start()
    for copy in stores:
        copy.wait()


def finish(at, place, rows, base, deep, groups):
    tok_rows, token_slots = place.shape
    width = rows.shape[1]
    share = base.shape[2] // deep
    steps = deep // max(1, LANES // share)
    return pl.pallas_call(
        functools.partial(finish_kernel, share, groups),
        in_specs=[
            pl.BlockSpec(memory_space=pltpu.SMEM),
            pl.BlockSpec(memory_space=pltpu.VMEM),
            pl.BlockSpec(memory_space=pl.ANY),
            pl.BlockSpec(memory_space=pl.ANY),
        ],
        out_specs=pl.BlockSpec(memory_space=pl.ANY),
        out_shape=jax.ShapeDtypeStruct((tok_rows, width), jnp.bfloat16),
        scratch_shapes=[
            pltpu.VMEM(rows.shape, jnp.bfloat16),
            pltpu.VMEM(base.shape, jnp.bfloat16),
            pltpu.VMEM((tok_rows, width), jnp.bfloat16),
            pltpu.SemaphoreType.DMA((3 * steps,)),
        ],
        compiler_params=pltpu.CompilerParams(vmem_limit_bytes=VMEM),
        cost_estimate=pl.CostEstimate(
            flops=2 * tok_rows * token_slots * width,
            bytes_accessed=2 * width * (token_slots + 2 * tok_rows),
            transcendentals=0,
        ),
    )(at, place, rows, base)


def local(activations, cotangent, family, value_weight, adapter_down, adapter_up):
    count = lax.axis_size("adapter")
    groups = lax.axis_size("groups")
    inner = PLANE // groups
    deep = count // inner
    tok_rows, width = activations.shape
    cap = max(2, (2 * tok_rows + count - 1) // count)
    token_slots = count * cap
    me = lax.axis_index("adapter")
    my_group = lax.axis_index("groups")
    my_inner = lax.rem(me, inner)
    my_layer = me // inner

    def next_layer(block, step):
        pairs = [(j, j + step) for j in range(count) if 0 <= j + step < count]
        return lax.ppermute(block, "adapter", pairs)

    def send_layers(block, layers):
        pairs = [(j * inner + at, k * inner + at) for j, k in layers for at in range(inner)]
        return lax.ppermute(block, "adapter", pairs)

    def pick(layer, *blocks):
        return lax.select_n(layer, *blocks)

    def around_groups(block, shift):
        pairs = [(j, (j + shift) % groups) for j in range(groups)]
        return lax.ppermute(block, "groups", pairs)

    def around_plane(block, shift):
        pairs = [
            (line * inner + j, line * inner + (j + shift) % inner)
            for line in range(deep)
            for j in range(inner)
        ]
        return lax.ppermute(block, "adapter", pairs)

    share = value_weight.shape[0] // groups
    own_share = lax.dynamic_slice_in_dim(value_weight, my_group * share, share, 0)
    family, own_share = lax.optimization_barrier((family, own_share))
    hops = [next_layer(own_share, inner), next_layer(own_share, -inner)]
    if deep == 4:
        hops.append(send_layers(own_share, ((0, 2), (3, 1))))
    else:
        for step in range(2, deep):
            hops += [next_layer(own_share, step * inner), next_layer(own_share, -step * inner)]

    send, place, back_place = pack(family, cotangent, cap, token_slots)
    received = lax.all_to_all(send, "adapter", split_axis=0, concat_axis=0, tiled=True)
    send_x = dot(place, activations, ((1,), (0,))).astype(jnp.bfloat16)
    send_x, hops, cotangent = lax.optimization_barrier((send_x, hops, cotangent))
    received_input = lax.all_to_all(send_x, "adapter", split_axis=0, concat_axis=0, tiled=True)

    plane_dy = [cotangent] + [around_groups(cotangent, -shift) for shift in range(1, groups)]
    plane_dy = jnp.stack(plane_dy)
    plane_dy = [plane_dy] + [around_plane(plane_dy, -shift) for shift in range(1, inner)]
    adapter_rows, backward_rows = make_rows(received, adapter_up, adapter_down)

    below, above = hops[:2]
    if deep == 4:
        lower = my_layer < 2
        over = hops[2]
        pair = jnp.concatenate([jnp.where(lower, above, over), jnp.where(lower, over, below)], axis=0)
        hops.append(send_layers(pair, ((1, 0), (2, 3))))
    received_input, adapter_rows, plane_dy, hops = lax.optimization_barrier(
        (received_input, adapter_rows, plane_dy, hops)
    )
    returned_rows = lax.all_to_all(adapter_rows, "adapter", split_axis=0, concat_axis=0, tiled=True)
    if deep == 4:
        below, above, over, pair = hops
        first, second = pair[:share], pair[share:]
        plane_weight = jnp.concatenate(
            [
                pick(my_layer, own_share, below, over, first),
                pick(my_layer, above, own_share, below, second),
                pick(my_layer, first, above, own_share, below),
                pick(my_layer, second, over, above, own_share),
            ],
            axis=0,
        )
    else:
        plane_weight = lax.dynamic_slice_in_dim(
            jnp.concatenate(hops[0::2][::-1] + [own_share] + hops[1::2], axis=0),
            (deep - 1 - my_layer) * share,
            deep * share,
            0,
        )
    plane_dy = [jnp.concatenate([d[s] for d in plane_dy], axis=0) for s in range(groups)]

    blocks = [dot(block, plane_weight, ((1,), (1,))).astype(jnp.bfloat16) for block in plane_dy]
    blocks = blocks[:1] + [around_groups(block, s) for s, block in enumerate(blocks) if s]
    received_input, blocks = lax.optimization_barrier((received_input, blocks))
    base = []
    for shift in range(inner):
        for block in blocks:
            piece = block[shift * tok_rows : (shift + 1) * tok_rows]
            base.append(around_plane(piece, shift) if shift else piece)
    base = jnp.stack(base)
    grad_down, grad_up = make_grads(
        received_input, received, backward_rows, adapter_up, adapter_down
    )
    at = jnp.stack([my_inner, my_group]).astype(jnp.int32)
    input_gradient = finish(at, back_place, returned_rows, base, deep, groups)
    return (input_gradient, grad_down, grad_up)


def solution(mesh):
    in_specs = (
        P(("groups", "adapter"), None),
        P(("groups", "adapter"), None),
        P(("groups", "adapter")),
        P("adapter", None),
        P(None, "adapter"),
        P("adapter", None),
    )
    out_specs = (P(("groups", "adapter"), None), P("groups", "adapter"), P("adapter", "groups"))
    return jax.shard_map(local, mesh=mesh, in_specs=in_specs, out_specs=out_specs, check_vma=False)
```

```python
import functools

import jax
import jax.numpy as jnp
from jax import lax
from jax.experimental import pallas as pl
from jax.experimental.pallas import tpu as pltpu
from jax.sharding import PartitionSpec as P

ADAPTER_RANK = 64
FAM_DEV = 8
PLANE = 8
LANES = 128
BLOCK = 1024
VMEM = 60 << 20


SCALE = 2.0


def dot(a, b, dims):
    return lax.dot_general(a, b, (dims, ((), ())), preferred_element_type=jnp.float32)


def pack_kernel(cap, family_ref, dy_ref, out_ref, place_ref, back_place_ref):
    tok_rows, features = dy_ref.shape
    token_slots = out_ref.shape[0]
    square = (tok_rows, tok_rows)
    along = jnp.broadcast_to(family_ref[...], square)
    down = along.T
    same = (along // FAM_DEV) == (down // FAM_DEV)
    row = lax.broadcasted_iota(jnp.int32, square, 0)
    column = lax.broadcasted_iota(jnp.int32, square, 1)
    rank_down = jnp.sum((same & (column < row)).astype(jnp.int32), axis=1, keepdims=True)
    rank_along = jnp.sum((same & (row < column)).astype(jnp.int32), axis=0, keepdims=True)
    slot_down = (down[:, :1] // FAM_DEV) * cap + rank_down
    slot_along = (along[:1] // FAM_DEV) * cap + rank_along
    slots = lax.broadcasted_iota(jnp.int32, (token_slots, tok_rows), 0)
    place = jnp.where(slots == slot_along, 1.0, 0.0).astype(jnp.bfloat16)
    place_ref[...] = place
    slots = lax.broadcasted_iota(jnp.int32, (tok_rows, token_slots), 1)
    back_place_ref[...] = jnp.where(slots == slot_down, 1.0, 0.0).astype(jnp.bfloat16)
    out_ref[:, :features] = dot(place, dy_ref[...], ((1,), (0,))).astype(jnp.bfloat16)
    families = (down % FAM_DEV).astype(jnp.float32)[:, :LANES].astype(jnp.bfloat16)
    out_ref[:, features:] = dot(place, families, ((1,), (0,))).astype(jnp.bfloat16)


def pack(family, cotangent, cap, token_slots):
    tok_rows, features = cotangent.shape
    return pl.pallas_call(
        functools.partial(pack_kernel, cap),
        out_shape=[
            jax.ShapeDtypeStruct((token_slots, features + LANES), jnp.bfloat16),
            jax.ShapeDtypeStruct((token_slots, tok_rows), jnp.bfloat16),
            jax.ShapeDtypeStruct((tok_rows, token_slots), jnp.bfloat16),
        ],
        compiler_params=pltpu.CompilerParams(vmem_limit_bytes=VMEM),
    )(family.reshape(1, tok_rows), cotangent)


def own_columns(family_ref, columns):
    shape = (family_ref.shape[0], columns)
    column_family = lax.broadcasted_iota(jnp.int32, shape, 1) // ADAPTER_RANK
    return column_family == family_ref[:, :1].astype(jnp.int32)


def rows_kernel(
    received_ref, up_ref, down_ref, rows_ref, backward_ref, dy, families, up, down, rows, sems
):
    width, columns = down.shape
    features = dy.shape[1]
    steps = width // BLOCK
    first = [
        pltpu.make_async_copy(received_ref.at[:, pl.ds(0, features)], dy, sems.at[0]),
        pltpu.make_async_copy(up_ref, up, sems.at[1]),
        pltpu.make_async_copy(
            received_ref.at[:, pl.ds(features, LANES)], families, sems.at[2]
        ),
    ]
    loads, stores = [], []
    for step in range(steps):
        part = pl.ds(step * BLOCK, BLOCK)
        loads.append(pltpu.make_async_copy(down_ref.at[part], down.at[part], sems.at[3 + step]))
        stores.append(
            pltpu.make_async_copy(
                rows.at[:, part], rows_ref.at[:, part], sems.at[3 + steps + step]
            )
        )
    for copy in first + loads:
        copy.start()
    for copy in first:
        copy.wait()
    back = dot(dy[...], up[...], ((1,), (1,)))
    back = jnp.where(own_columns(families, columns), back, 0.0).astype(jnp.bfloat16)
    backward_ref[...] = back
    for step in range(steps):
        part = pl.ds(step * BLOCK, BLOCK)
        loads[step].wait()
        product = dot(back, down[part], ((1,), (1,)))
        rows[:, part] = (SCALE * product).astype(jnp.bfloat16)
        stores[step].start()
    for copy in stores:
        copy.wait()


def make_rows(received, adapter_up, adapter_down):
    token_slots = received.shape[0]
    columns, features = adapter_up.shape
    width = adapter_down.shape[0]
    return pl.pallas_call(
        rows_kernel,
        in_specs=[pl.BlockSpec(memory_space=pl.ANY)] * 3,
        out_specs=[
            pl.BlockSpec(memory_space=pl.ANY),
            pl.BlockSpec(memory_space=pltpu.VMEM),
        ],
        out_shape=[
            jax.ShapeDtypeStruct((token_slots, width), jnp.bfloat16),
            jax.ShapeDtypeStruct((token_slots, columns), jnp.bfloat16),
        ],
        scratch_shapes=[
            pltpu.VMEM((token_slots, features), jnp.bfloat16),
            pltpu.VMEM((token_slots, LANES), jnp.bfloat16),
            pltpu.VMEM((columns, features), jnp.bfloat16),
            pltpu.VMEM((width, columns), jnp.bfloat16),
            pltpu.VMEM((token_slots, width), jnp.bfloat16),
            pltpu.SemaphoreType.DMA((3 + 2 * (width // BLOCK),)),
        ],
        compiler_params=pltpu.CompilerParams(vmem_limit_bytes=VMEM),
        cost_estimate=pl.CostEstimate(
            flops=2 * token_slots * columns * (width + features),
            bytes_accessed=2 * (columns + token_slots) * (width + features),
            transcendentals=0,
        ),
    )(received, adapter_up, adapter_down)


def grads_kernel(x_ref, dy_ref, family_ref, backward_ref, down_ref, grad_down_ref, grad_up_ref, low_ref):
    step = pl.program_id(0)

    @pl.when(step == 0)
    def _():
        low_ref[...] = jnp.zeros_like(low_ref)

    low_ref[...] += dot(x_ref[...], down_ref[...], ((1,), (0,)))
    grad_down = dot(x_ref[...], backward_ref[...], ((0,), (0,)))
    grad_down_ref[...] = (SCALE * grad_down).astype(jnp.bfloat16)

    @pl.when(step == pl.num_programs(0) - 1)
    def _():
        keep = own_columns(family_ref, low_ref.shape[1])
        low = jnp.where(keep, low_ref[...], 0.0).astype(jnp.bfloat16)
        grad_up = dot(low, dy_ref[...], ((0,), (0,)))
        grad_up_ref[...] = (SCALE * grad_up).astype(jnp.bfloat16)


def make_grads(received_input, received, backward_rows, adapter_up, adapter_down):
    token_slots = received.shape[0]
    columns, features = adapter_up.shape
    width = adapter_down.shape[0]
    return pl.pallas_call(
        grads_kernel,
        grid=(width // BLOCK,),
        in_specs=[
            pl.BlockSpec((token_slots, BLOCK), lambda j: (0, j)),
            pl.BlockSpec((token_slots, features), lambda j: (0, 0)),
            pl.BlockSpec((token_slots, LANES), lambda j: (0, features // LANES)),
            pl.BlockSpec((token_slots, columns), lambda j: (0, 0)),
            pl.BlockSpec((BLOCK, columns), lambda j: (j, 0)),
        ],
        out_specs=[
            pl.BlockSpec((BLOCK, columns), lambda j: (j, 0)),
            pl.BlockSpec((columns, features), lambda j: (0, 0)),
        ],
        out_shape=[
            jax.ShapeDtypeStruct((width, columns), jnp.bfloat16),
            jax.ShapeDtypeStruct((columns, features), jnp.bfloat16),
        ],
        scratch_shapes=[pltpu.VMEM((token_slots, columns), jnp.float32)],
        compiler_params=pltpu.CompilerParams(vmem_limit_bytes=VMEM),
        cost_estimate=pl.CostEstimate(
            flops=2 * token_slots * columns * (2 * width + features),
            bytes_accessed=2 * (2 * columns + token_slots) * (width + features),
            transcendentals=0,
        ),
    )(received_input, received, received, backward_rows, adapter_down)


def finish_kernel(
    share, groups, at_ref, place_ref, rows_ref, base_ref, out_ref, rows, base, out, sems
):
    inner = PLANE // groups
    wide = PLANE * share
    layers = max(1, LANES // share)
    steps = base.shape[2] // (layers * share)
    loads, stores = [], []
    for step in range(steps):
        part = pl.ds(step * layers * wide, layers * wide)
        side = pl.ds(step * layers * share, layers * share)
        loads.append(
            (
                pltpu.make_async_copy(base_ref.at[:, :, side], base.at[:, :, side], sems.at[step]),
                pltpu.make_async_copy(
                    rows_ref.at[:, part], rows.at[:, part], sems.at[steps + step]
                ),
            )
        )
        stores.append(
            pltpu.make_async_copy(
                out.at[:, part], out_ref.at[:, part], sems.at[2 * steps + step]
            )
        )
    for pair in loads:
        for copy in pair:
            copy.start()
    for step in range(steps):
        for copy in loads[step]:
            copy.wait()
        for layer in range(step * layers, (step + 1) * layers):
            for block in range(PLANE):
                columns = pl.ds((layer * PLANE + block) * share, share)
                adapter_part = dot(place_ref[...], rows[:, columns], ((1,), (0,)))
                inner_shift = lax.rem(at_ref[0] - block // groups + inner, inner)
                group_shift = lax.rem(at_ref[1] - block % groups + groups, groups)
                frozen_part = base[inner_shift * groups + group_shift]
                frozen_part = frozen_part[:, layer * share : (layer + 1) * share]
                total = frozen_part.astype(jnp.float32) + adapter_part
                out[:, columns] = total.astype(jnp.bfloat16)
        stores[step].start()
    for copy in stores:
        copy.wait()


def finish(at, place, rows, base, deep, groups):
    tok_rows, token_slots = place.shape
    width = rows.shape[1]
    share = base.shape[2] // deep
    steps = deep // max(1, LANES // share)
    return pl.pallas_call(
        functools.partial(finish_kernel, share, groups),
        in_specs=[
            pl.BlockSpec(memory_space=pltpu.SMEM),
            pl.BlockSpec(memory_space=pltpu.VMEM),
            pl.BlockSpec(memory_space=pl.ANY),
            pl.BlockSpec(memory_space=pl.ANY),
        ],
        out_specs=pl.BlockSpec(memory_space=pl.ANY),
        out_shape=jax.ShapeDtypeStruct((tok_rows, width), jnp.bfloat16),
        scratch_shapes=[
            pltpu.VMEM(rows.shape, jnp.bfloat16),
            pltpu.VMEM(base.shape, jnp.bfloat16),
            pltpu.VMEM((tok_rows, width), jnp.bfloat16),
            pltpu.SemaphoreType.DMA((3 * steps,)),
        ],
        compiler_params=pltpu.CompilerParams(vmem_limit_bytes=VMEM),
        cost_estimate=pl.CostEstimate(
            flops=2 * tok_rows * token_slots * width,
            bytes_accessed=2 * width * (token_slots + 2 * tok_rows),
            transcendentals=0,
        ),
    )(at, place, rows, base)


def local(activations, cotangent, family, value_weight, adapter_down, adapter_up):
    count = lax.axis_size("adapter")
    groups = lax.axis_size("groups")
    inner = PLANE // groups
    deep = count // inner
    tok_rows, width = activations.shape
    cap = max(2, (2 * tok_rows + count - 1) // count)
    token_slots = count * cap
    me = lax.axis_index("adapter")
    my_group = lax.axis_index("groups")
    my_inner = lax.rem(me, inner)
    my_layer = me // inner

    def next_layer(block, step):
        pairs = [(j, j + step) for j in range(count) if 0 <= j + step < count]
        return lax.ppermute(block, "adapter", pairs)

    def send_layers(block, layers):
        pairs = [(j * inner + at, k * inner + at) for j, k in layers for at in range(inner)]
        return lax.ppermute(block, "adapter", pairs)

    def pick(layer, *blocks):
        return lax.select_n(layer, *blocks)

    def around_groups(block, shift):
        pairs = [(j, (j + shift) % groups) for j in range(groups)]
        return lax.ppermute(block, "groups", pairs)

    def around_plane(block, shift):
        pairs = [
            (line * inner + j, line * inner + (j + shift) % inner)
            for line in range(deep)
            for j in range(inner)
        ]
        return lax.ppermute(block, "adapter", pairs)

    share = value_weight.shape[0] // groups
    own_share = lax.dynamic_slice_in_dim(value_weight, my_group * share, share, 0)
    family, own_share = lax.optimization_barrier((family, own_share))
    hops = [next_layer(own_share, inner), next_layer(own_share, -inner)]
    if deep == 4:
        hops.append(send_layers(own_share, ((0, 2), (3, 1))))
    else:
        for step in range(2, deep):
            hops += [next_layer(own_share, step * inner), next_layer(own_share, -step * inner)]

    send, place, back_place = pack(family, cotangent, cap, token_slots)
    received = lax.all_to_all(send, "adapter", split_axis=0, concat_axis=0, tiled=True)
    below, above = hops[:2]
    if deep == 4:
        lower = my_layer < 2
        over = hops[2]
        pair = jnp.concatenate([jnp.where(lower, above, over), jnp.where(lower, over, below)], axis=0)
        hops.append(pair)
    place, hops, cotangent = lax.optimization_barrier((place, hops, cotangent))
    send_x = dot(place, activations, ((1,), (0,))).astype(jnp.bfloat16)
    received_input = lax.all_to_all(send_x, "adapter", split_axis=0, concat_axis=0, tiled=True)

    plane_dy = [cotangent] + [around_groups(cotangent, -shift) for shift in range(1, groups)]
    plane_dy = jnp.stack(plane_dy)
    plane_dy = [plane_dy] + [around_plane(plane_dy, -shift) for shift in range(1, inner)]
    adapter_rows, backward_rows = make_rows(received, adapter_up, adapter_down)

    if deep == 4:
        hops[3] = send_layers(hops[3], ((1, 0), (2, 3)))
    received_input, adapter_rows, plane_dy, hops = lax.optimization_barrier(
        (received_input, adapter_rows, plane_dy, hops)
    )
    returned_rows = lax.all_to_all(adapter_rows, "adapter", split_axis=0, concat_axis=0, tiled=True)
    if deep == 4:
        below, above, over, pair = hops
        first, second = pair[:share], pair[share:]
        plane_weight = jnp.concatenate(
            [
                pick(my_layer, own_share, below, over, first),
                pick(my_layer, above, own_share, below, second),
                pick(my_layer, first, above, own_share, below),
                pick(my_layer, second, over, above, own_share),
            ],
            axis=0,
        )
    else:
        plane_weight = lax.dynamic_slice_in_dim(
            jnp.concatenate(hops[0::2][::-1] + [own_share] + hops[1::2], axis=0),
            (deep - 1 - my_layer) * share,
            deep * share,
            0,
        )
    plane_dy = [jnp.concatenate([d[s] for d in plane_dy], axis=0) for s in range(groups)]

    blocks = [dot(block, plane_weight, ((1,), (1,))).astype(jnp.bfloat16) for block in plane_dy]
    blocks = blocks[:1] + [around_groups(block, s) for s, block in enumerate(blocks) if s]
    received_input, blocks = lax.optimization_barrier((received_input, blocks))
    base = []
    for shift in range(inner):
        for block in blocks:
            piece = block[shift * tok_rows : (shift + 1) * tok_rows]
            base.append(around_plane(piece, shift) if shift else piece)
    base = jnp.stack(base)
    grad_down, grad_up = make_grads(
        received_input, received, backward_rows, adapter_up, adapter_down
    )
    at = jnp.stack([my_inner, my_group]).astype(jnp.int32)
    input_gradient = finish(at, back_place, returned_rows, base, deep, groups)
    return (input_gradient, grad_down, grad_up)


def solution(mesh):
    in_specs = (
        P(("groups", "adapter"), None),
        P(("groups", "adapter"), None),
        P(("groups", "adapter")),
        P("adapter", None),
        P(None, "adapter"),
        P("adapter", None),
    )
    out_specs = (P(("groups", "adapter"), None), P("groups", "adapter"), P("adapter", "groups"))
    return jax.shard_map(local, mesh=mesh, in_specs=in_specs, out_specs=out_specs, check_vma=False)
```

```python
import functools

import jax
import jax.numpy as jnp
from jax import lax
from jax.experimental import pallas as pl
from jax.experimental.pallas import tpu as pltpu
from jax.sharding import PartitionSpec as P

ADAPTER_RANK = 64
FAM_DEV = 8
PLANE = 8
LANES = 128
BLOCK = 1024
VMEM = 60 << 20
PAIR_FLOPS = 100_000_000_000


SCALE = 2.0


def dot(a, b, dims):
    return lax.dot_general(a, b, (dims, ((), ())), preferred_element_type=jnp.float32)


def pack_kernel(cap, family_ref, dy_ref, out_ref, place_ref, back_place_ref):
    tok_rows, features = dy_ref.shape
    token_slots = out_ref.shape[0]
    square = (tok_rows, tok_rows)
    along = jnp.broadcast_to(family_ref[...], square)
    down = along.T
    same = (along // FAM_DEV) == (down // FAM_DEV)
    row = lax.broadcasted_iota(jnp.int32, square, 0)
    column = lax.broadcasted_iota(jnp.int32, square, 1)
    rank_down = jnp.sum((same & (column < row)).astype(jnp.int32), axis=1, keepdims=True)
    rank_along = jnp.sum((same & (row < column)).astype(jnp.int32), axis=0, keepdims=True)
    slot_down = (down[:, :1] // FAM_DEV) * cap + rank_down
    slot_along = (along[:1] // FAM_DEV) * cap + rank_along
    slots = lax.broadcasted_iota(jnp.int32, (token_slots, tok_rows), 0)
    place = jnp.where(slots == slot_along, 1.0, 0.0).astype(jnp.bfloat16)
    place_ref[...] = place
    slots = lax.broadcasted_iota(jnp.int32, (tok_rows, token_slots), 1)
    back_place_ref[...] = jnp.where(slots == slot_down, 1.0, 0.0).astype(jnp.bfloat16)
    out_ref[:, :features] = dot(place, dy_ref[...], ((1,), (0,))).astype(jnp.bfloat16)
    families = (down % FAM_DEV).astype(jnp.float32)[:, :LANES].astype(jnp.bfloat16)
    out_ref[:, features:] = dot(place, families, ((1,), (0,))).astype(jnp.bfloat16)


def pack(family, cotangent, cap, token_slots):
    tok_rows, features = cotangent.shape
    return pl.pallas_call(
        functools.partial(pack_kernel, cap),
        out_shape=[
            jax.ShapeDtypeStruct((token_slots, features + LANES), jnp.bfloat16),
            jax.ShapeDtypeStruct((token_slots, tok_rows), jnp.bfloat16),
            jax.ShapeDtypeStruct((tok_rows, token_slots), jnp.bfloat16),
        ],
        compiler_params=pltpu.CompilerParams(vmem_limit_bytes=VMEM),
    )(family.reshape(1, tok_rows), cotangent)


def pack_x_kernel(place_ref, x_ref, out_ref):
    out_ref[...] = dot(place_ref[...], x_ref[...], ((1,), (0,))).astype(jnp.bfloat16)


def pack_x(place, activations):
    token_slots, tok_rows = place.shape
    width = activations.shape[1]
    columns = 2 * BLOCK
    return pl.pallas_call(
        pack_x_kernel,
        grid=(width // columns,),
        in_specs=[
            pl.BlockSpec((token_slots, tok_rows), lambda j: (0, 0)),
            pl.BlockSpec((tok_rows, columns), lambda j: (0, j)),
        ],
        out_specs=pl.BlockSpec((token_slots, columns), lambda j: (0, j)),
        out_shape=jax.ShapeDtypeStruct((token_slots, width), jnp.bfloat16),
        compiler_params=pltpu.CompilerParams(vmem_limit_bytes=VMEM),
        cost_estimate=pl.CostEstimate(
            flops=2 * tok_rows * token_slots * width,
            bytes_accessed=2 * width * (token_slots + tok_rows),
            transcendentals=0,
        ),
    )(place, activations)


def own_columns(family_ref, columns):
    shape = (family_ref.shape[0], columns)
    column_family = lax.broadcasted_iota(jnp.int32, shape, 1) // ADAPTER_RANK
    return column_family == family_ref[:, :1].astype(jnp.int32)


def rows_kernel(
    received_ref, up_ref, down_ref, rows_ref, backward_ref, dy, families, up, down, rows, sems
):
    width, columns = down.shape
    features = dy.shape[1]
    steps = width // BLOCK
    first = [
        pltpu.make_async_copy(received_ref.at[:, pl.ds(0, features)], dy, sems.at[0]),
        pltpu.make_async_copy(up_ref, up, sems.at[1]),
        pltpu.make_async_copy(
            received_ref.at[:, pl.ds(features, LANES)], families, sems.at[2]
        ),
    ]
    loads, stores = [], []
    for step in range(steps):
        part = pl.ds(step * BLOCK, BLOCK)
        loads.append(pltpu.make_async_copy(down_ref.at[part], down.at[part], sems.at[3 + step]))
        stores.append(
            pltpu.make_async_copy(
                rows.at[:, part], rows_ref.at[:, part], sems.at[3 + steps + step]
            )
        )
    for copy in first + loads:
        copy.start()
    for copy in first:
        copy.wait()
    back = dot(dy[...], up[...], ((1,), (1,)))
    back = jnp.where(own_columns(families, columns), back, 0.0).astype(jnp.bfloat16)
    backward_ref[...] = back
    for step in range(steps):
        part = pl.ds(step * BLOCK, BLOCK)
        loads[step].wait()
        product = dot(back, down[part], ((1,), (1,)))
        rows[:, part] = (SCALE * product).astype(jnp.bfloat16)
        stores[step].start()
    for copy in stores:
        copy.wait()


def make_rows(received, adapter_up, adapter_down):
    token_slots = received.shape[0]
    columns, features = adapter_up.shape
    width = adapter_down.shape[0]
    return pl.pallas_call(
        rows_kernel,
        in_specs=[pl.BlockSpec(memory_space=pl.ANY)] * 3,
        out_specs=[
            pl.BlockSpec(memory_space=pl.ANY),
            pl.BlockSpec(memory_space=pltpu.VMEM),
        ],
        out_shape=[
            jax.ShapeDtypeStruct((token_slots, width), jnp.bfloat16),
            jax.ShapeDtypeStruct((token_slots, columns), jnp.bfloat16),
        ],
        scratch_shapes=[
            pltpu.VMEM((token_slots, features), jnp.bfloat16),
            pltpu.VMEM((token_slots, LANES), jnp.bfloat16),
            pltpu.VMEM((columns, features), jnp.bfloat16),
            pltpu.VMEM((width, columns), jnp.bfloat16),
            pltpu.VMEM((token_slots, width), jnp.bfloat16),
            pltpu.SemaphoreType.DMA((3 + 2 * (width // BLOCK),)),
        ],
        compiler_params=pltpu.CompilerParams(vmem_limit_bytes=VMEM),
        cost_estimate=pl.CostEstimate(
            flops=2 * token_slots * columns * (width + features),
            bytes_accessed=2 * (columns + token_slots) * (width + features),
            transcendentals=0,
        ),
    )(received, adapter_up, adapter_down)


def grads_kernel(x_ref, dy_ref, family_ref, backward_ref, down_ref, grad_down_ref, grad_up_ref, low_ref):
    step = pl.program_id(0)

    @pl.when(step == 0)
    def _():
        low_ref[...] = jnp.zeros_like(low_ref)

    low_ref[...] += dot(x_ref[...], down_ref[...], ((1,), (0,)))
    grad_down = dot(x_ref[...], backward_ref[...], ((0,), (0,)))
    grad_down_ref[...] = (SCALE * grad_down).astype(jnp.bfloat16)

    @pl.when(step == pl.num_programs(0) - 1)
    def _():
        keep = own_columns(family_ref, low_ref.shape[1])
        low = jnp.where(keep, low_ref[...], 0.0).astype(jnp.bfloat16)
        grad_up = dot(low, dy_ref[...], ((0,), (0,)))
        grad_up_ref[...] = (SCALE * grad_up).astype(jnp.bfloat16)


def make_grads(received_input, received, backward_rows, adapter_up, adapter_down):
    token_slots = received.shape[0]
    columns, features = adapter_up.shape
    width = adapter_down.shape[0]
    return pl.pallas_call(
        grads_kernel,
        grid=(width // BLOCK,),
        in_specs=[
            pl.BlockSpec((token_slots, BLOCK), lambda j: (0, j)),
            pl.BlockSpec((token_slots, features), lambda j: (0, 0)),
            pl.BlockSpec((token_slots, LANES), lambda j: (0, features // LANES)),
            pl.BlockSpec((token_slots, columns), lambda j: (0, 0)),
            pl.BlockSpec((BLOCK, columns), lambda j: (j, 0)),
        ],
        out_specs=[
            pl.BlockSpec((BLOCK, columns), lambda j: (j, 0)),
            pl.BlockSpec((columns, features), lambda j: (0, 0)),
        ],
        out_shape=[
            jax.ShapeDtypeStruct((width, columns), jnp.bfloat16),
            jax.ShapeDtypeStruct((columns, features), jnp.bfloat16),
        ],
        scratch_shapes=[pltpu.VMEM((token_slots, columns), jnp.float32)],
        compiler_params=pltpu.CompilerParams(vmem_limit_bytes=VMEM),
        cost_estimate=pl.CostEstimate(
            flops=2 * token_slots * columns * (2 * width + features),
            bytes_accessed=2 * (2 * columns + token_slots) * (width + features),
            transcendentals=0,
        ),
    )(received_input, received, received, backward_rows, adapter_down)


def finish_kernel(
    share, groups, at_ref, place_ref, rows_ref, base_ref, out_ref, rows, base, out, sems
):
    inner = PLANE // groups
    wide = PLANE * share
    layers = max(1, LANES // share)
    steps = base.shape[2] // (layers * share)
    loads, stores = [], []
    for step in range(steps):
        part = pl.ds(step * layers * wide, layers * wide)
        side = pl.ds(step * layers * share, layers * share)
        loads.append(
            (
                pltpu.make_async_copy(base_ref.at[:, :, side], base.at[:, :, side], sems.at[step]),
                pltpu.make_async_copy(
                    rows_ref.at[:, part], rows.at[:, part], sems.at[steps + step]
                ),
            )
        )
        stores.append(
            pltpu.make_async_copy(
                out.at[:, part], out_ref.at[:, part], sems.at[2 * steps + step]
            )
        )
    for pair in loads:
        for copy in pair:
            copy.start()
    for step in range(steps):
        for copy in loads[step]:
            copy.wait()
        for layer in range(step * layers, (step + 1) * layers):
            for block in range(PLANE):
                columns = pl.ds((layer * PLANE + block) * share, share)
                adapter_part = dot(place_ref[...], rows[:, columns], ((1,), (0,)))
                inner_shift = lax.rem(at_ref[0] - block // groups + inner, inner)
                group_shift = lax.rem(at_ref[1] - block % groups + groups, groups)
                frozen_part = base[inner_shift * groups + group_shift]
                frozen_part = frozen_part[:, layer * share : (layer + 1) * share]
                total = frozen_part.astype(jnp.float32) + adapter_part
                out[:, columns] = total.astype(jnp.bfloat16)
        stores[step].start()
    for copy in stores:
        copy.wait()


def finish(at, place, rows, base, deep, groups):
    tok_rows, token_slots = place.shape
    width = rows.shape[1]
    share = base.shape[2] // deep
    steps = deep // max(1, LANES // share)
    return pl.pallas_call(
        functools.partial(finish_kernel, share, groups),
        in_specs=[
            pl.BlockSpec(memory_space=pltpu.SMEM),
            pl.BlockSpec(memory_space=pltpu.VMEM),
            pl.BlockSpec(memory_space=pl.ANY),
            pl.BlockSpec(memory_space=pl.ANY),
        ],
        out_specs=pl.BlockSpec(memory_space=pl.ANY),
        out_shape=jax.ShapeDtypeStruct((tok_rows, width), jnp.bfloat16),
        scratch_shapes=[
            pltpu.VMEM(rows.shape, jnp.bfloat16),
            pltpu.VMEM(base.shape, jnp.bfloat16),
            pltpu.VMEM((tok_rows, width), jnp.bfloat16),
            pltpu.SemaphoreType.DMA((3 * steps,)),
        ],
        compiler_params=pltpu.CompilerParams(vmem_limit_bytes=VMEM),
        cost_estimate=pl.CostEstimate(
            flops=2 * tok_rows * token_slots * width,
            bytes_accessed=2 * width * (token_slots + 2 * tok_rows),
            transcendentals=0,
        ),
    )(at, place, rows, base)


def pair_kernel(layer_ref, below_ref, above_ref, over_ref, out_ref):
    share = below_ref.shape[0]

    @pl.when(layer_ref[0] < 2)
    def _():
        out_ref[:share] = above_ref[...]
        out_ref[share:] = over_ref[...]

    @pl.when(layer_ref[0] >= 2)
    def _():
        out_ref[:share] = over_ref[...]
        out_ref[share:] = below_ref[...]


def make_pair(layer, below, above, over):
    share, features = below.shape
    whole = pl.BlockSpec(memory_space=pltpu.VMEM)
    return pl.pallas_call(
        pair_kernel,
        in_specs=[pl.BlockSpec(memory_space=pltpu.SMEM), whole, whole, whole],
        out_specs=whole,
        out_shape=jax.ShapeDtypeStruct((2 * share, features), jnp.bfloat16),
        cost_estimate=pl.CostEstimate(
            flops=PAIR_FLOPS, bytes_accessed=10 * share * features, transcendentals=0
        ),
    )(layer[None], below, above, over)


def local(activations, cotangent, family, value_weight, adapter_down, adapter_up):
    count = lax.axis_size("adapter")
    groups = lax.axis_size("groups")
    inner = PLANE // groups
    deep = count // inner
    tok_rows, width = activations.shape
    cap = max(2, (2 * tok_rows + count - 1) // count)
    token_slots = count * cap
    me = lax.axis_index("adapter")
    my_group = lax.axis_index("groups")
    my_inner = lax.rem(me, inner)
    my_layer = me // inner

    def next_layer(block, step):
        pairs = [(j, j + step) for j in range(count) if 0 <= j + step < count]
        return lax.ppermute(block, "adapter", pairs)

    def send_layers(block, layers):
        pairs = [(j * inner + at, k * inner + at) for j, k in layers for at in range(inner)]
        return lax.ppermute(block, "adapter", pairs)

    def pick(layer, *blocks):
        return lax.select_n(layer, *blocks)

    def around_groups(block, shift):
        pairs = [(j, (j + shift) % groups) for j in range(groups)]
        return lax.ppermute(block, "groups", pairs)

    def around_plane(block, shift):
        pairs = [
            (line * inner + j, line * inner + (j + shift) % inner)
            for line in range(deep)
            for j in range(inner)
        ]
        return lax.ppermute(block, "adapter", pairs)

    share = value_weight.shape[0] // groups
    own_share = lax.dynamic_slice_in_dim(value_weight, my_group * share, share, 0)
    family, own_share = lax.optimization_barrier((family, own_share))
    hops = [next_layer(own_share, inner), next_layer(own_share, -inner)]
    if deep > 4:
        for step in range(2, deep):
            hops += [next_layer(own_share, step * inner), next_layer(own_share, -step * inner)]

    send, place, back_place = pack(family, cotangent, cap, token_slots)
    received = lax.all_to_all(send, "adapter", split_axis=0, concat_axis=0, tiled=True)
    send_x = pack_x(place, activations)
    received, own_share, cotangent, send_x = lax.optimization_barrier(
        (received, own_share, cotangent, send_x)
    )
    if deep == 4:
        hops.append(send_layers(own_share, ((0, 2), (3, 1))))
    received_input = lax.all_to_all(send_x, "adapter", split_axis=0, concat_axis=0, tiled=True)

    plane_dy = [cotangent] + [around_groups(cotangent, -shift) for shift in range(1, groups)]
    plane_dy = jnp.stack(plane_dy)
    plane_dy = [plane_dy] + [around_plane(plane_dy, -shift) for shift in range(1, inner)]
    adapter_rows, backward_rows = make_rows(received, adapter_up, adapter_down)

    if deep == 4:
        hops.append(send_layers(make_pair(my_layer, *hops), ((1, 0), (2, 3))))
    received_input, adapter_rows, plane_dy, hops = lax.optimization_barrier(
        (received_input, adapter_rows, plane_dy, hops)
    )
    returned_rows = lax.all_to_all(adapter_rows, "adapter", split_axis=0, concat_axis=0, tiled=True)
    if deep == 4:
        below, above, over, pair = hops
        first, second = pair[:share], pair[share:]
        plane_weight = jnp.concatenate(
            [
                pick(my_layer, own_share, below, over, first),
                pick(my_layer, above, own_share, below, second),
                pick(my_layer, first, above, own_share, below),
                pick(my_layer, second, over, above, own_share),
            ],
            axis=0,
        )
    else:
        plane_weight = lax.dynamic_slice_in_dim(
            jnp.concatenate(hops[0::2][::-1] + [own_share] + hops[1::2], axis=0),
            (deep - 1 - my_layer) * share,
            deep * share,
            0,
        )
    plane_dy = [jnp.concatenate([d[s] for d in plane_dy], axis=0) for s in range(groups)]

    blocks = [dot(block, plane_weight, ((1,), (1,))).astype(jnp.bfloat16) for block in plane_dy]
    blocks = blocks[:1] + [around_groups(block, s) for s, block in enumerate(blocks) if s]
    base = []
    for shift in range(inner):
        for block in blocks:
            piece = block[shift * tok_rows : (shift + 1) * tok_rows]
            base.append(around_plane(piece, shift) if shift else piece)
    base = jnp.stack(base)
    received_input, base = lax.optimization_barrier((received_input, base))
    grad_down, grad_up = make_grads(
        received_input, received, backward_rows, adapter_up, adapter_down
    )
    at = jnp.stack([my_inner, my_group]).astype(jnp.int32)
    input_gradient = finish(at, back_place, returned_rows, base, deep, groups)
    return (input_gradient, grad_down, grad_up)


def solution(mesh):
    in_specs = (
        P(("groups", "adapter"), None),
        P(("groups", "adapter"), None),
        P(("groups", "adapter")),
        P("adapter", None),
        P(None, "adapter"),
        P("adapter", None),
    )
    out_specs = (P(("groups", "adapter"), None), P("groups", "adapter"), P("adapter", "groups"))
    return jax.shard_map(local, mesh=mesh, in_specs=in_specs, out_specs=out_specs, check_vma=False)
```

```python
import functools

import jax
import jax.numpy as jnp
from jax import lax
from jax.experimental import pallas as pl
from jax.experimental.pallas import tpu as pltpu
from jax.sharding import PartitionSpec as P

ADAPTER_RANK = 64
FAM_DEV = 8
PLANE = 8
LANES = 128
BLOCK = 1024
VMEM = 60 << 20
PAIR_FLOPS = 100_000_000_000


SCALE = 2.0


def dot(a, b, dims):
    return lax.dot_general(a, b, (dims, ((), ())), preferred_element_type=jnp.float32)


def pack_kernel(cap, family_ref, dy_ref, out_ref, place_ref, back_place_ref):
    tok_rows, features = dy_ref.shape
    token_slots = out_ref.shape[0]
    square = (tok_rows, tok_rows)
    along = jnp.broadcast_to(family_ref[...], square)
    down = along.T
    same = (along // FAM_DEV) == (down // FAM_DEV)
    row = lax.broadcasted_iota(jnp.int32, square, 0)
    column = lax.broadcasted_iota(jnp.int32, square, 1)
    rank_down = jnp.sum((same & (column < row)).astype(jnp.int32), axis=1, keepdims=True)
    rank_along = jnp.sum((same & (row < column)).astype(jnp.int32), axis=0, keepdims=True)
    slot_down = (down[:, :1] // FAM_DEV) * cap + rank_down
    slot_along = (along[:1] // FAM_DEV) * cap + rank_along
    slots = lax.broadcasted_iota(jnp.int32, (token_slots, tok_rows), 0)
    place = jnp.where(slots == slot_along, 1.0, 0.0).astype(jnp.bfloat16)
    place_ref[...] = place
    slots = lax.broadcasted_iota(jnp.int32, (tok_rows, token_slots), 1)
    back_place_ref[...] = jnp.where(slots == slot_down, 1.0, 0.0).astype(jnp.bfloat16)
    out_ref[:, :features] = dot(place, dy_ref[...], ((1,), (0,))).astype(jnp.bfloat16)
    families = (down % FAM_DEV).astype(jnp.float32)[:, :LANES].astype(jnp.bfloat16)
    out_ref[:, features:] = dot(place, families, ((1,), (0,))).astype(jnp.bfloat16)


def pack(family, cotangent, cap, token_slots):
    tok_rows, features = cotangent.shape
    return pl.pallas_call(
        functools.partial(pack_kernel, cap),
        out_shape=[
            jax.ShapeDtypeStruct((token_slots, features + LANES), jnp.bfloat16),
            jax.ShapeDtypeStruct((token_slots, tok_rows), jnp.bfloat16),
            jax.ShapeDtypeStruct((tok_rows, token_slots), jnp.bfloat16),
        ],
        compiler_params=pltpu.CompilerParams(vmem_limit_bytes=VMEM),
    )(family.reshape(1, tok_rows), cotangent)


def pack_x_kernel(place_ref, x_ref, out_ref):
    out_ref[...] = dot(place_ref[...], x_ref[...], ((1,), (0,))).astype(jnp.bfloat16)


def pack_x(place, activations):
    token_slots, tok_rows = place.shape
    width = activations.shape[1]
    columns = 2 * BLOCK
    return pl.pallas_call(
        pack_x_kernel,
        grid=(width // columns,),
        in_specs=[
            pl.BlockSpec((token_slots, tok_rows), lambda j: (0, 0)),
            pl.BlockSpec((tok_rows, columns), lambda j: (0, j)),
        ],
        out_specs=pl.BlockSpec((token_slots, columns), lambda j: (0, j)),
        out_shape=jax.ShapeDtypeStruct((token_slots, width), jnp.bfloat16),
        compiler_params=pltpu.CompilerParams(vmem_limit_bytes=VMEM),
        cost_estimate=pl.CostEstimate(
            flops=2 * tok_rows * token_slots * width,
            bytes_accessed=2 * width * (token_slots + tok_rows),
            transcendentals=0,
        ),
    )(place, activations)


def own_columns(family_ref, columns):
    shape = (family_ref.shape[0], columns)
    column_family = lax.broadcasted_iota(jnp.int32, shape, 1) // ADAPTER_RANK
    return column_family == family_ref[:, :1].astype(jnp.int32)


def rows_kernel(
    received_ref, up_ref, down_ref, rows_ref, backward_ref, dy, families, up, down, rows, sems
):
    width, columns = down.shape
    features = dy.shape[1]
    steps = width // BLOCK
    first = [
        pltpu.make_async_copy(received_ref.at[:, pl.ds(0, features)], dy, sems.at[0]),
        pltpu.make_async_copy(up_ref, up, sems.at[1]),
        pltpu.make_async_copy(
            received_ref.at[:, pl.ds(features, LANES)], families, sems.at[2]
        ),
    ]
    loads, stores = [], []
    for step in range(steps):
        part = pl.ds(step * BLOCK, BLOCK)
        loads.append(pltpu.make_async_copy(down_ref.at[part], down.at[part], sems.at[3 + step]))
        stores.append(
            pltpu.make_async_copy(
                rows.at[:, part], rows_ref.at[:, part], sems.at[3 + steps + step]
            )
        )
    for copy in first + loads:
        copy.start()
    for copy in first:
        copy.wait()
    back = dot(dy[...], up[...], ((1,), (1,)))
    back = jnp.where(own_columns(families, columns), back, 0.0).astype(jnp.bfloat16)
    backward_ref[...] = back
    for step in range(steps):
        part = pl.ds(step * BLOCK, BLOCK)
        loads[step].wait()
        product = dot(back, down[part], ((1,), (1,)))
        rows[:, part] = (SCALE * product).astype(jnp.bfloat16)
        stores[step].start()
    for copy in stores:
        copy.wait()


def make_rows(received, adapter_up, adapter_down):
    token_slots = received.shape[0]
    columns, features = adapter_up.shape
    width = adapter_down.shape[0]
    return pl.pallas_call(
        rows_kernel,
        in_specs=[pl.BlockSpec(memory_space=pl.ANY)] * 3,
        out_specs=[
            pl.BlockSpec(memory_space=pl.ANY),
            pl.BlockSpec(memory_space=pltpu.VMEM),
        ],
        out_shape=[
            jax.ShapeDtypeStruct((token_slots, width), jnp.bfloat16),
            jax.ShapeDtypeStruct((token_slots, columns), jnp.bfloat16),
        ],
        scratch_shapes=[
            pltpu.VMEM((token_slots, features), jnp.bfloat16),
            pltpu.VMEM((token_slots, LANES), jnp.bfloat16),
            pltpu.VMEM((columns, features), jnp.bfloat16),
            pltpu.VMEM((width, columns), jnp.bfloat16),
            pltpu.VMEM((token_slots, width), jnp.bfloat16),
            pltpu.SemaphoreType.DMA((3 + 2 * (width // BLOCK),)),
        ],
        compiler_params=pltpu.CompilerParams(vmem_limit_bytes=VMEM),
        cost_estimate=pl.CostEstimate(
            flops=2 * token_slots * columns * (width + features),
            bytes_accessed=2 * (columns + token_slots) * (width + features),
            transcendentals=0,
        ),
    )(received, adapter_up, adapter_down)


def grads_kernel(x_ref, dy_ref, family_ref, backward_ref, down_ref, grad_down_ref, grad_up_ref, low_ref):
    step = pl.program_id(0)

    @pl.when(step == 0)
    def _():
        low_ref[...] = jnp.zeros_like(low_ref)

    low_ref[...] += dot(x_ref[...], down_ref[...], ((1,), (0,)))
    grad_down = dot(x_ref[...], backward_ref[...], ((0,), (0,)))
    grad_down_ref[...] = (SCALE * grad_down).astype(jnp.bfloat16)

    @pl.when(step == pl.num_programs(0) - 1)
    def _():
        keep = own_columns(family_ref, low_ref.shape[1])
        low = jnp.where(keep, low_ref[...], 0.0).astype(jnp.bfloat16)
        grad_up = dot(low, dy_ref[...], ((0,), (0,)))
        grad_up_ref[...] = (SCALE * grad_up).astype(jnp.bfloat16)


def make_grads(received_input, received, backward_rows, adapter_up, adapter_down):
    token_slots = received.shape[0]
    columns, features = adapter_up.shape
    width = adapter_down.shape[0]
    return pl.pallas_call(
        grads_kernel,
        grid=(width // BLOCK,),
        in_specs=[
            pl.BlockSpec((token_slots, BLOCK), lambda j: (0, j)),
            pl.BlockSpec((token_slots, features), lambda j: (0, 0)),
            pl.BlockSpec((token_slots, LANES), lambda j: (0, features // LANES)),
            pl.BlockSpec((token_slots, columns), lambda j: (0, 0)),
            pl.BlockSpec((BLOCK, columns), lambda j: (j, 0)),
        ],
        out_specs=[
            pl.BlockSpec((BLOCK, columns), lambda j: (j, 0)),
            pl.BlockSpec((columns, features), lambda j: (0, 0)),
        ],
        out_shape=[
            jax.ShapeDtypeStruct((width, columns), jnp.bfloat16),
            jax.ShapeDtypeStruct((columns, features), jnp.bfloat16),
        ],
        scratch_shapes=[pltpu.VMEM((token_slots, columns), jnp.float32)],
        compiler_params=pltpu.CompilerParams(vmem_limit_bytes=VMEM // 2),
        cost_estimate=pl.CostEstimate(
            flops=2 * token_slots * columns * (2 * width + features),
            bytes_accessed=2 * (2 * columns + token_slots) * (width + features),
            transcendentals=0,
        ),
    )(received_input, received, received, backward_rows, adapter_down)


def finish_kernel(
    share, groups, at_ref, place_ref, rows_ref, base, out_ref, rows, out, sems
):
    inner = PLANE // groups
    wide = PLANE * share
    layers = max(1, LANES // share)
    steps = base.shape[2] // (layers * share)
    loads, stores = [], []
    for step in range(steps):
        part = pl.ds(step * layers * wide, layers * wide)
        loads.append(
            pltpu.make_async_copy(rows_ref.at[:, part], rows.at[:, part], sems.at[step])
        )
        stores.append(
            pltpu.make_async_copy(
                out.at[:, part], out_ref.at[:, part], sems.at[steps + step]
            )
        )
    for copy in loads:
        copy.start()
    for step in range(steps):
        loads[step].wait()
        for layer in range(step * layers, (step + 1) * layers):
            for block in range(PLANE):
                columns = pl.ds((layer * PLANE + block) * share, share)
                adapter_part = dot(place_ref[...], rows[:, columns], ((1,), (0,)))
                inner_shift = lax.rem(at_ref[0] - block // groups + inner, inner)
                group_shift = lax.rem(at_ref[1] - block % groups + groups, groups)
                frozen_part = base[inner_shift * groups + group_shift]
                frozen_part = frozen_part[:, layer * share : (layer + 1) * share]
                total = frozen_part.astype(jnp.float32) + adapter_part
                out[:, columns] = total.astype(jnp.bfloat16)
        stores[step].start()
    for copy in stores:
        copy.wait()


def finish(at, place, rows, base, deep, groups):
    tok_rows, token_slots = place.shape
    width = rows.shape[1]
    share = base.shape[2] // deep
    steps = deep // max(1, LANES // share)
    return pl.pallas_call(
        functools.partial(finish_kernel, share, groups),
        in_specs=[
            pl.BlockSpec(memory_space=pltpu.SMEM),
            pl.BlockSpec(memory_space=pltpu.VMEM),
            pl.BlockSpec(memory_space=pl.ANY),
            pl.BlockSpec(memory_space=pltpu.VMEM),
        ],
        out_specs=pl.BlockSpec(memory_space=pl.ANY),
        out_shape=jax.ShapeDtypeStruct((tok_rows, width), jnp.bfloat16),
        scratch_shapes=[
            pltpu.VMEM(rows.shape, jnp.bfloat16),
            pltpu.VMEM((tok_rows, width), jnp.bfloat16),
            pltpu.SemaphoreType.DMA((2 * steps,)),
        ],
        compiler_params=pltpu.CompilerParams(vmem_limit_bytes=VMEM // 2),
        cost_estimate=pl.CostEstimate(
            flops=2 * tok_rows * token_slots * width,
            bytes_accessed=2 * width * (token_slots + 2 * tok_rows),
            transcendentals=0,
        ),
    )(at, place, rows, base)


def pair_kernel(layer_ref, below_ref, above_ref, over_ref, out_ref):
    share = below_ref.shape[0]

    @pl.when(layer_ref[0] < 2)
    def _():
        out_ref[:share] = above_ref[...]
        out_ref[share:] = over_ref[...]

    @pl.when(layer_ref[0] >= 2)
    def _():
        out_ref[:share] = over_ref[...]
        out_ref[share:] = below_ref[...]


def make_pair(layer, below, above, over):
    share, features = below.shape
    whole = pl.BlockSpec(memory_space=pltpu.VMEM)
    return pl.pallas_call(
        pair_kernel,
        in_specs=[pl.BlockSpec(memory_space=pltpu.SMEM), whole, whole, whole],
        out_specs=whole,
        out_shape=jax.ShapeDtypeStruct((2 * share, features), jnp.bfloat16),
        cost_estimate=pl.CostEstimate(
            flops=PAIR_FLOPS, bytes_accessed=10 * share * features, transcendentals=0
        ),
    )(layer[None], below, above, over)


def local(activations, cotangent, family, value_weight, adapter_down, adapter_up):
    count = lax.axis_size("adapter")
    groups = lax.axis_size("groups")
    inner = PLANE // groups
    deep = count // inner
    tok_rows, width = activations.shape
    cap = max(2, (2 * tok_rows + count - 1) // count)
    token_slots = count * cap
    me = lax.axis_index("adapter")
    my_group = lax.axis_index("groups")
    my_inner = lax.rem(me, inner)
    my_layer = me // inner

    def next_layer(block, step):
        pairs = [(j, j + step) for j in range(count) if 0 <= j + step < count]
        return lax.ppermute(block, "adapter", pairs)

    def send_layers(block, layers):
        pairs = [(j * inner + at, k * inner + at) for j, k in layers for at in range(inner)]
        return lax.ppermute(block, "adapter", pairs)

    def pick(layer, *blocks):
        return lax.select_n(layer, *blocks)

    def around_groups(block, shift):
        pairs = [(j, (j + shift) % groups) for j in range(groups)]
        return lax.ppermute(block, "groups", pairs)

    def around_plane(block, shift):
        pairs = [
            (line * inner + j, line * inner + (j + shift) % inner)
            for line in range(deep)
            for j in range(inner)
        ]
        return lax.ppermute(block, "adapter", pairs)

    share = value_weight.shape[0] // groups
    own_share = lax.dynamic_slice_in_dim(value_weight, my_group * share, share, 0)
    family, own_share = lax.optimization_barrier((family, own_share))
    hops = [next_layer(own_share, inner), next_layer(own_share, -inner)]
    if deep > 4:
        for step in range(2, deep):
            hops += [next_layer(own_share, step * inner), next_layer(own_share, -step * inner)]

    send, place, back_place = pack(family, cotangent, cap, token_slots)
    received = lax.all_to_all(send, "adapter", split_axis=0, concat_axis=0, tiled=True)
    send_x = pack_x(place, activations)
    received, own_share, cotangent, send_x = lax.optimization_barrier(
        (received, own_share, cotangent, send_x)
    )
    if deep == 4:
        hops.append(send_layers(own_share, ((0, 2), (3, 1))))
    received_input = lax.all_to_all(send_x, "adapter", split_axis=0, concat_axis=0, tiled=True)

    plane_dy = [cotangent] + [around_groups(cotangent, -shift) for shift in range(1, groups)]
    plane_dy = jnp.stack(plane_dy)
    plane_dy = [plane_dy] + [around_plane(plane_dy, -shift) for shift in range(1, inner)]
    adapter_rows, backward_rows = make_rows(received, adapter_up, adapter_down)

    if deep == 4:
        hops.append(send_layers(make_pair(my_layer, *hops), ((1, 0), (2, 3))))
    received_input, adapter_rows, plane_dy, hops = lax.optimization_barrier(
        (received_input, adapter_rows, plane_dy, hops)
    )
    returned_rows = lax.all_to_all(adapter_rows, "adapter", split_axis=0, concat_axis=0, tiled=True)
    if deep == 4:
        below, above, over, pair = hops
        first, second = pair[:share], pair[share:]
        plane_weight = jnp.concatenate(
            [
                pick(my_layer, own_share, below, over, first),
                pick(my_layer, above, own_share, below, second),
                pick(my_layer, first, above, own_share, below),
                pick(my_layer, second, over, above, own_share),
            ],
            axis=0,
        )
    else:
        plane_weight = lax.dynamic_slice_in_dim(
            jnp.concatenate(hops[0::2][::-1] + [own_share] + hops[1::2], axis=0),
            (deep - 1 - my_layer) * share,
            deep * share,
            0,
        )
    plane_dy = [jnp.concatenate([d[s] for d in plane_dy], axis=0) for s in range(groups)]

    blocks = [dot(block, plane_weight, ((1,), (1,))).astype(jnp.bfloat16) for block in plane_dy]
    blocks = blocks[:1] + [around_groups(block, s) for s, block in enumerate(blocks) if s]
    base = []
    for shift in range(inner):
        for block in blocks:
            piece = block[shift * tok_rows : (shift + 1) * tok_rows]
            base.append(around_plane(piece, shift) if shift else piece)
    base = jnp.stack(base)
    received_input, base = lax.optimization_barrier((received_input, base))
    grad_down, grad_up = make_grads(
        received_input, received, backward_rows, adapter_up, adapter_down
    )
    at = jnp.stack([my_inner, my_group]).astype(jnp.int32)
    input_gradient = finish(at, back_place, returned_rows, base, deep, groups)
    return (input_gradient, grad_down, grad_up)


def solution(mesh):
    in_specs = (
        P(("groups", "adapter"), None),
        P(("groups", "adapter"), None),
        P(("groups", "adapter")),
        P("adapter", None),
        P(None, "adapter"),
        P("adapter", None),
    )
    out_specs = (P(("groups", "adapter"), None), P("groups", "adapter"), P("adapter", "groups"))
    return jax.shard_map(local, mesh=mesh, in_specs=in_specs, out_specs=out_specs, check_vma=False)
```

```python
import functools

import jax
import jax.numpy as jnp
from jax import lax
from jax.experimental import pallas as pl
from jax.experimental.pallas import tpu as pltpu
from jax.sharding import PartitionSpec as P

ADAPTER_RANK = 64
FAM_DEV = 8
PLANE = 8
LANES = 128
BLOCK = 1024
VMEM = 60 << 20
EARLY_FLOPS = 100_000_000_000


SCALE = 2.0


def dot(a, b, dims):
    return lax.dot_general(a, b, (dims, ((), ())), preferred_element_type=jnp.float32)


def pack_kernel(cap, family_ref, dy_ref, out_ref, place_ref, back_place_ref):
    tok_rows, features = dy_ref.shape
    token_slots = out_ref.shape[0]
    square = (tok_rows, tok_rows)
    along = jnp.broadcast_to(family_ref[...], square)
    down = along.T
    same = (along // FAM_DEV) == (down // FAM_DEV)
    row = lax.broadcasted_iota(jnp.int32, square, 0)
    column = lax.broadcasted_iota(jnp.int32, square, 1)
    rank_down = jnp.sum((same & (column < row)).astype(jnp.int32), axis=1, keepdims=True)
    rank_along = jnp.sum((same & (row < column)).astype(jnp.int32), axis=0, keepdims=True)
    slot_down = (down[:, :1] // FAM_DEV) * cap + rank_down
    slot_along = (along[:1] // FAM_DEV) * cap + rank_along
    slots = lax.broadcasted_iota(jnp.int32, (token_slots, tok_rows), 0)
    place = jnp.where(slots == slot_along, 1.0, 0.0).astype(jnp.bfloat16)
    place_ref[...] = place
    slots = lax.broadcasted_iota(jnp.int32, (tok_rows, token_slots), 1)
    back_place_ref[...] = jnp.where(slots == slot_down, 1.0, 0.0).astype(jnp.bfloat16)
    out_ref[:, :features] = dot(place, dy_ref[...], ((1,), (0,))).astype(jnp.bfloat16)
    families = (down % FAM_DEV).astype(jnp.float32)[:, :LANES].astype(jnp.bfloat16)
    out_ref[:, features:] = dot(place, families, ((1,), (0,))).astype(jnp.bfloat16)


def pack(family, cotangent, cap, token_slots):
    tok_rows, features = cotangent.shape
    return pl.pallas_call(
        functools.partial(pack_kernel, cap),
        out_shape=[
            jax.ShapeDtypeStruct((token_slots, features + LANES), jnp.bfloat16),
            jax.ShapeDtypeStruct((token_slots, tok_rows), jnp.bfloat16),
            jax.ShapeDtypeStruct((tok_rows, token_slots), jnp.bfloat16),
        ],
        compiler_params=pltpu.CompilerParams(vmem_limit_bytes=VMEM),
    )(family.reshape(1, tok_rows), cotangent)


def pack_x_kernel(place_ref, x_ref, out_ref):
    out_ref[...] = dot(place_ref[...], x_ref[...], ((1,), (0,))).astype(jnp.bfloat16)


def pack_x(place, activations, columns):
    token_slots, tok_rows = place.shape
    width = activations.shape[1] if columns is None else columns
    step = width // 2
    return pl.pallas_call(
        pack_x_kernel,
        grid=(2,),
        in_specs=[
            pl.BlockSpec((token_slots, tok_rows), lambda j: (0, 0)),
            pl.BlockSpec((tok_rows, step), lambda j: (0, j)),
        ],
        out_specs=pl.BlockSpec((token_slots, step), lambda j: (0, j)),
        out_shape=jax.ShapeDtypeStruct((token_slots, width), jnp.bfloat16),
        compiler_params=pltpu.CompilerParams(vmem_limit_bytes=VMEM),
        cost_estimate=pl.CostEstimate(
            flops=2 * tok_rows * token_slots * width,
            bytes_accessed=2 * width * (token_slots + tok_rows),
            transcendentals=0,
        ),
    )(place, activations)


def own_columns(family_ref, columns):
    shape = (family_ref.shape[0], columns)
    column_family = lax.broadcasted_iota(jnp.int32, shape, 1) // ADAPTER_RANK
    return column_family == family_ref[:, :1].astype(jnp.int32)


def rows_kernel(
    received_ref, up_ref, down_ref, rows_ref, backward_ref, dy, families, up, down, rows, sems
):
    width, columns = down.shape
    features = dy.shape[1]
    steps = width // BLOCK
    first = [
        pltpu.make_async_copy(received_ref.at[:, pl.ds(0, features)], dy, sems.at[0]),
        pltpu.make_async_copy(up_ref, up, sems.at[1]),
        pltpu.make_async_copy(
            received_ref.at[:, pl.ds(features, LANES)], families, sems.at[2]
        ),
    ]
    loads, stores = [], []
    for step in range(steps):
        part = pl.ds(step * BLOCK, BLOCK)
        loads.append(pltpu.make_async_copy(down_ref.at[part], down.at[part], sems.at[3 + step]))
        stores.append(
            pltpu.make_async_copy(
                rows.at[:, part], rows_ref.at[:, part], sems.at[3 + steps + step]
            )
        )
    for copy in first + loads:
        copy.start()
    for copy in first:
        copy.wait()
    back = dot(dy[...], up[...], ((1,), (1,)))
    back = jnp.where(own_columns(families, columns), back, 0.0).astype(jnp.bfloat16)
    backward_ref[...] = back
    for step in range(steps):
        part = pl.ds(step * BLOCK, BLOCK)
        loads[step].wait()
        product = dot(back, down[part], ((1,), (1,)))
        rows[:, part] = (SCALE * product).astype(jnp.bfloat16)
        stores[step].start()
    for copy in stores:
        copy.wait()


def make_rows(received, adapter_up, adapter_down):
    token_slots = received.shape[0]
    columns, features = adapter_up.shape
    width = adapter_down.shape[0]
    return pl.pallas_call(
        rows_kernel,
        in_specs=[pl.BlockSpec(memory_space=pl.ANY)] * 3,
        out_specs=[
            pl.BlockSpec(memory_space=pl.ANY),
            pl.BlockSpec(memory_space=pltpu.VMEM),
        ],
        out_shape=[
            jax.ShapeDtypeStruct((token_slots, width), jnp.bfloat16),
            jax.ShapeDtypeStruct((token_slots, columns), jnp.bfloat16),
        ],
        scratch_shapes=[
            pltpu.VMEM((token_slots, features), jnp.bfloat16),
            pltpu.VMEM((token_slots, LANES), jnp.bfloat16),
            pltpu.VMEM((columns, features), jnp.bfloat16),
            pltpu.VMEM((width, columns), jnp.bfloat16),
            pltpu.VMEM((token_slots, width), jnp.bfloat16),
            pltpu.SemaphoreType.DMA((3 + 2 * (width // BLOCK),)),
        ],
        compiler_params=pltpu.CompilerParams(vmem_limit_bytes=VMEM),
        cost_estimate=pl.CostEstimate(
            flops=2 * token_slots * columns * (width + features),
            bytes_accessed=2 * (columns + token_slots) * (width + features),
            transcendentals=0,
        ),
    )(received, adapter_up, adapter_down)


def grads_kernel(pieces, *refs):
    dy_ref, family_ref, backward_ref, down_ref, grad_down_ref, grad_up_ref, low_ref = refs[pieces:]
    step = pl.program_id(0)
    x = refs[0][...]
    if pieces == 2:
        x = jnp.where(step < pl.num_programs(0) - 1, x, refs[1][...])

    @pl.when(step == 0)
    def _():
        low_ref[...] = jnp.zeros_like(low_ref)

    low_ref[...] += dot(x, down_ref[...], ((1,), (0,)))
    grad_down = dot(x, backward_ref[...], ((0,), (0,)))
    grad_down_ref[...] = (SCALE * grad_down).astype(jnp.bfloat16)

    @pl.when(step == pl.num_programs(0) - 1)
    def _():
        keep = own_columns(family_ref, low_ref.shape[1])
        low = jnp.where(keep, low_ref[...], 0.0).astype(jnp.bfloat16)
        grad_up = dot(low, dy_ref[...], ((0,), (0,)))
        grad_up_ref[...] = (SCALE * grad_up).astype(jnp.bfloat16)


def make_grads(xs, received, backward_rows, adapter_up, adapter_down):
    token_slots = received.shape[0]
    columns, features = adapter_up.shape
    width = adapter_down.shape[0]
    blocks = xs[0].shape[1] // BLOCK
    return pl.pallas_call(
        functools.partial(grads_kernel, len(xs)),
        grid=(width // BLOCK,),
        in_specs=[
            pl.BlockSpec((token_slots, BLOCK), lambda j: (0, jnp.minimum(j, blocks - 1))),
            *[pl.BlockSpec((token_slots, BLOCK), lambda j: (0, 0)) for _ in xs[1:]],
            pl.BlockSpec((token_slots, features), lambda j: (0, 0)),
            pl.BlockSpec((token_slots, LANES), lambda j: (0, features // LANES)),
            pl.BlockSpec((token_slots, columns), lambda j: (0, 0)),
            pl.BlockSpec((BLOCK, columns), lambda j: (j, 0)),
        ],
        out_specs=[
            pl.BlockSpec((BLOCK, columns), lambda j: (j, 0)),
            pl.BlockSpec((columns, features), lambda j: (0, 0)),
        ],
        out_shape=[
            jax.ShapeDtypeStruct((width, columns), jnp.bfloat16),
            jax.ShapeDtypeStruct((columns, features), jnp.bfloat16),
        ],
        scratch_shapes=[pltpu.VMEM((token_slots, columns), jnp.float32)],
        compiler_params=pltpu.CompilerParams(vmem_limit_bytes=VMEM // 2),
        cost_estimate=pl.CostEstimate(
            flops=2 * token_slots * columns * (2 * width + features),
            bytes_accessed=2 * (2 * columns + token_slots) * (width + features),
            transcendentals=0,
        ),
    )(*xs, received, received, backward_rows, adapter_down)


def finish_kernel(
    share, groups, at_ref, place_ref, rows_ref, base, out_ref, rows, out, sems
):
    inner = PLANE // groups
    wide = PLANE * share
    layers = max(1, LANES // share)
    steps = base.shape[2] // (layers * share)
    loads, stores = [], []
    for step in range(steps):
        part = pl.ds(step * layers * wide, layers * wide)
        loads.append(
            pltpu.make_async_copy(rows_ref.at[:, part], rows.at[:, part], sems.at[step])
        )
        stores.append(
            pltpu.make_async_copy(
                out.at[:, part], out_ref.at[:, part], sems.at[steps + step]
            )
        )
    for copy in loads:
        copy.start()
    for step in range(steps):
        loads[step].wait()
        for layer in range(step * layers, (step + 1) * layers):
            for block in range(PLANE):
                columns = pl.ds((layer * PLANE + block) * share, share)
                adapter_part = dot(place_ref[...], rows[:, columns], ((1,), (0,)))
                inner_shift = lax.rem(at_ref[0] - block // groups + inner, inner)
                group_shift = lax.rem(at_ref[1] - block % groups + groups, groups)
                frozen_part = base[inner_shift * groups + group_shift]
                frozen_part = frozen_part[:, layer * share : (layer + 1) * share]
                total = frozen_part.astype(jnp.float32) + adapter_part
                out[:, columns] = total.astype(jnp.bfloat16)
        stores[step].start()
    for copy in stores:
        copy.wait()


def finish(at, place, rows, base, deep, groups):
    tok_rows, token_slots = place.shape
    width = rows.shape[1]
    share = base.shape[2] // deep
    steps = deep // max(1, LANES // share)
    return pl.pallas_call(
        functools.partial(finish_kernel, share, groups),
        in_specs=[
            pl.BlockSpec(memory_space=pltpu.SMEM),
            pl.BlockSpec(memory_space=pltpu.VMEM),
            pl.BlockSpec(memory_space=pl.ANY),
            pl.BlockSpec(memory_space=pltpu.VMEM),
        ],
        out_specs=pl.BlockSpec(memory_space=pl.ANY),
        out_shape=jax.ShapeDtypeStruct((tok_rows, width), jnp.bfloat16),
        scratch_shapes=[
            pltpu.VMEM(rows.shape, jnp.bfloat16),
            pltpu.VMEM((tok_rows, width), jnp.bfloat16),
            pltpu.SemaphoreType.DMA((2 * steps,)),
        ],
        compiler_params=pltpu.CompilerParams(vmem_limit_bytes=VMEM // 2),
        cost_estimate=pl.CostEstimate(
            flops=2 * tok_rows * token_slots * width,
            bytes_accessed=2 * width * (token_slots + 2 * tok_rows),
            transcendentals=0,
        ),
    )(at, place, rows, base)


def pair_kernel(layer_ref, below_ref, above_ref, over_ref, out_ref):
    share = below_ref.shape[0]

    @pl.when(layer_ref[0] < 2)
    def _():
        out_ref[:share] = above_ref[...]
        out_ref[share:] = over_ref[...]

    @pl.when(layer_ref[0] >= 2)
    def _():
        out_ref[:share] = over_ref[...]
        out_ref[share:] = below_ref[...]


def make_pair(layer, below, above, over):
    share, features = below.shape
    whole = pl.BlockSpec(memory_space=pltpu.VMEM)
    return pl.pallas_call(
        pair_kernel,
        in_specs=[pl.BlockSpec(memory_space=pltpu.SMEM), whole, whole, whole],
        out_specs=whole,
        out_shape=jax.ShapeDtypeStruct((2 * share, features), jnp.bfloat16),
        cost_estimate=pl.CostEstimate(
            flops=EARLY_FLOPS, bytes_accessed=10 * share * features, transcendentals=0
        ),
    )(layer[None], below, above, over)


def to_owners_kernel(rows, at_ref, *refs):
    count = len(refs) // 2
    for turn in range(count):
        start = pl.multiple_of(lax.bitwise_xor(at_ref[0], turn) * rows, rows)
        for block in range(count):
            refs[count + turn][block * rows : (block + 1) * rows] = refs[block][
                pl.ds(start, rows)
            ]


def to_owners(at, blocks):
    whole = pl.BlockSpec(memory_space=pltpu.VMEM)
    return pl.pallas_call(
        functools.partial(to_owners_kernel, blocks[0].shape[0] // len(blocks)),
        in_specs=[pl.BlockSpec(memory_space=pltpu.SMEM)] + [whole] * len(blocks),
        out_specs=[whole] * len(blocks),
        out_shape=[jax.ShapeDtypeStruct(b.shape, b.dtype) for b in blocks],
        cost_estimate=pl.CostEstimate(
            flops=EARLY_FLOPS, bytes_accessed=4 * len(blocks) * blocks[0].size, transcendentals=0
        ),
    )(at, *blocks)


def by_sender_kernel(rows, at_ref, *refs):
    count = len(refs) - 1
    for turn in range(count):
        for block in range(count):
            layer = lax.bitwise_xor(at_ref[1], block)
            sender = layer * count + lax.bitwise_xor(at_ref[0], turn)
            start = pl.multiple_of(sender * rows, rows)
            refs[count][pl.ds(start, rows)] = refs[turn][block * rows : (block + 1) * rows]


def by_sender(at, blocks):
    whole = pl.BlockSpec(memory_space=pltpu.VMEM)
    slots, columns = blocks[0].shape
    return pl.pallas_call(
        functools.partial(by_sender_kernel, slots // len(blocks)),
        in_specs=[pl.BlockSpec(memory_space=pltpu.SMEM)] + [whole] * len(blocks),
        out_specs=whole,
        out_shape=jax.ShapeDtypeStruct((slots * len(blocks), columns), jnp.bfloat16),
    )(at, *blocks)


def local(activations, cotangent, family, value_weight, adapter_down, adapter_up):
    count = lax.axis_size("adapter")
    groups = lax.axis_size("groups")
    inner = PLANE // groups
    deep = count // inner
    tok_rows, width = activations.shape
    cap = max(2, (2 * tok_rows + count - 1) // count)
    token_slots = count * cap
    me = lax.axis_index("adapter")
    my_group = lax.axis_index("groups")
    my_inner = lax.rem(me, inner)
    my_layer = me // inner

    def next_layer(block, step):
        pairs = [(j, j + step) for j in range(count) if 0 <= j + step < count]
        return lax.ppermute(block, "adapter", pairs)

    def send_layers(block, layers):
        pairs = [(j * inner + at, k * inner + at) for j, k in layers for at in range(inner)]
        return lax.ppermute(block, "adapter", pairs)

    def turned(block, bits, step):
        pairs = [(j, (j // step ^ bits) * step + j % step) for j in range(count)]
        return lax.ppermute(block, "adapter", pairs)

    def pick(layer, *blocks):
        return lax.select_n(layer, *blocks)

    def around_groups(block, shift):
        pairs = [(j, (j + shift) % groups) for j in range(groups)]
        return lax.ppermute(block, "groups", pairs)

    def around_plane(block, shift):
        pairs = [
            (line * inner + j, line * inner + (j + shift) % inner)
            for line in range(deep)
            for j in range(inner)
        ]
        return lax.ppermute(block, "adapter", pairs)

    share = value_weight.shape[0] // groups
    own_share = lax.dynamic_slice_in_dim(value_weight, my_group * share, share, 0)
    family, own_share = lax.optimization_barrier((family, own_share))
    hops = [next_layer(own_share, inner), next_layer(own_share, -inner)]
    if deep > 4:
        for step in range(2, deep):
            hops += [next_layer(own_share, step * inner), next_layer(own_share, -step * inner)]

    send, place, back_place = pack(family, cotangent, cap, token_slots)
    received = lax.all_to_all(send, "adapter", split_axis=0, concat_axis=0, tiled=True)
    split = deep == inner == 4 and width > BLOCK
    send_x = pack_x(place, activations, width - BLOCK if split else None)
    received, own_share, cotangent, send_x = lax.optimization_barrier(
        (received, own_share, cotangent, send_x)
    )
    if deep == 4:
        hops.append(send_layers(own_share, ((0, 2), (3, 1))))
    received_input = lax.all_to_all(send_x, "adapter", split_axis=0, concat_axis=0, tiled=True)

    plane_dy = [cotangent] + [around_groups(cotangent, -shift) for shift in range(1, groups)]
    plane_dy = jnp.stack(plane_dy)
    plane_dy = [plane_dy] + [around_plane(plane_dy, -shift) for shift in range(1, inner)]
    adapter_rows, backward_rows = make_rows(received, adapter_up, adapter_down)

    if deep == 4:
        hops.append(send_layers(make_pair(my_layer, *hops), ((1, 0), (2, 3))))
    crossed = []
    if split:
        last = dot(place, activations[:, width - BLOCK :], ((1,), (0,))).astype(jnp.bfloat16)
        last, backward_rows = lax.optimization_barrier((last, backward_rows))
        slots = token_slots // deep
        for k in range(deep):
            start = lax.bitwise_xor(my_layer, jnp.int32(k)) * slots
            block = lax.dynamic_slice_in_dim(last, start, slots, 0)
            crossed.append(turned(block, k, inner) if k else block)
    received_input, adapter_rows, plane_dy, hops = lax.optimization_barrier(
        (received_input, adapter_rows, plane_dy, hops)
    )
    returned_rows = lax.all_to_all(adapter_rows, "adapter", split_axis=0, concat_axis=0, tiled=True)
    if deep == 4:
        below, above, over, pair = hops
        first, second = pair[:share], pair[share:]
        plane_weight = jnp.concatenate(
            [
                pick(my_layer, own_share, below, over, first),
                pick(my_layer, above, own_share, below, second),
                pick(my_layer, first, above, own_share, below),
                pick(my_layer, second, over, above, own_share),
            ],
            axis=0,
        )
    else:
        plane_weight = lax.dynamic_slice_in_dim(
            jnp.concatenate(hops[0::2][::-1] + [own_share] + hops[1::2], axis=0),
            (deep - 1 - my_layer) * share,
            deep * share,
            0,
        )
    plane_dy = [jnp.concatenate([d[s] for d in plane_dy], axis=0) for s in range(groups)]

    blocks = [dot(block, plane_weight, ((1,), (1,))).astype(jnp.bfloat16) for block in plane_dy]
    blocks = blocks[:1] + [around_groups(block, s) for s, block in enumerate(blocks) if s]
    at = jnp.stack([my_inner, my_layer]).astype(jnp.int32)
    xs = [received_input]
    if split:
        crossed = to_owners(at, crossed)
        crossed = [turned(block, k, 1) if k else block for k, block in enumerate(crossed)]
        xs.append(by_sender(at, crossed))
    base = []
    for shift in range(inner):
        for block in blocks:
            piece = block[shift * tok_rows : (shift + 1) * tok_rows]
            base.append(around_plane(piece, shift) if shift else piece)
    base = jnp.stack(base)
    xs, base = lax.optimization_barrier((xs, base))
    grad_down, grad_up = make_grads(
        xs, received, backward_rows, adapter_up, adapter_down
    )
    at = jnp.stack([my_inner, my_group]).astype(jnp.int32)
    input_gradient = finish(at, back_place, returned_rows, base, deep, groups)
    return (input_gradient, grad_down, grad_up)


def solution(mesh):
    in_specs = (
        P(("groups", "adapter"), None),
        P(("groups", "adapter"), None),
        P(("groups", "adapter")),
        P("adapter", None),
        P(None, "adapter"),
        P("adapter", None),
    )
    out_specs = (P(("groups", "adapter"), None), P("groups", "adapter"), P("adapter", "groups"))
    return jax.shard_map(local, mesh=mesh, in_specs=in_specs, out_specs=out_specs, check_vma=False)
```

```python
import functools

import jax
import jax.numpy as jnp
from jax import lax
from jax.experimental import pallas as pl
from jax.experimental.pallas import tpu as pltpu
from jax.sharding import PartitionSpec as P

ADAPTER_RANK = 64
FAM_DEV = 8
PLANE = 8
LANES = 128
BLOCK = 1024
VMEM = 60 << 20
EARLY_FLOPS = 100_000_000_000


SCALE = 2.0


def dot(a, b, dims):
    return lax.dot_general(a, b, (dims, ((), ())), preferred_element_type=jnp.float32)


def pack_kernel(cap, family_ref, dy_ref, out_ref, place_ref):
    tok_rows, features = dy_ref.shape
    token_slots = out_ref.shape[0]
    square = (tok_rows, tok_rows)
    along = jnp.broadcast_to(family_ref[...], square)
    down = along.T
    same = (along // FAM_DEV) == (down // FAM_DEV)
    row = lax.broadcasted_iota(jnp.int32, square, 0)
    column = lax.broadcasted_iota(jnp.int32, square, 1)
    rank = jnp.sum((same & (row < column)).astype(jnp.int32), axis=0, keepdims=True)
    slot = (along[:1] // FAM_DEV) * cap + rank
    slots = lax.broadcasted_iota(jnp.int32, (token_slots, tok_rows), 0)
    place = jnp.where(slots == slot, 1.0, 0.0).astype(jnp.bfloat16)
    place_ref[...] = place
    families = (down % FAM_DEV).astype(jnp.float32)[:, :LANES].astype(jnp.bfloat16)
    out_ref[:, features:] = dot(place, families, ((1,), (0,))).astype(jnp.bfloat16)
    out_ref[:, :features] = dot(place, dy_ref[...], ((1,), (0,))).astype(jnp.bfloat16)


def pack(family, cotangent, cap, token_slots):
    tok_rows, features = cotangent.shape
    whole = pl.BlockSpec(memory_space=pltpu.VMEM)
    return pl.pallas_call(
        functools.partial(pack_kernel, cap),
        in_specs=[whole, whole],
        out_specs=[whole, whole],
        out_shape=[
            jax.ShapeDtypeStruct((token_slots, features + LANES), jnp.bfloat16),
            jax.ShapeDtypeStruct((token_slots, tok_rows), jnp.bfloat16),
        ],
        compiler_params=pltpu.CompilerParams(vmem_limit_bytes=VMEM),
    )(family.reshape(1, tok_rows), cotangent)


def pack_x_kernel(place_ref, x_ref, out_ref):
    out_ref[...] = dot(place_ref[...], x_ref[...], ((1,), (0,))).astype(jnp.bfloat16)


def pack_x(place, activations, columns):
    token_slots, tok_rows = place.shape
    width = activations.shape[1] if columns is None else columns
    step = width // 2
    return pl.pallas_call(
        pack_x_kernel,
        grid=(2,),
        in_specs=[
            pl.BlockSpec((token_slots, tok_rows), lambda j: (0, 0)),
            pl.BlockSpec((tok_rows, step), lambda j: (0, j)),
        ],
        out_specs=pl.BlockSpec((token_slots, step), lambda j: (0, j)),
        out_shape=jax.ShapeDtypeStruct((token_slots, width), jnp.bfloat16),
        compiler_params=pltpu.CompilerParams(vmem_limit_bytes=VMEM),
        cost_estimate=pl.CostEstimate(
            flops=2 * tok_rows * token_slots * width,
            bytes_accessed=2 * width * (token_slots + tok_rows),
            transcendentals=0,
        ),
    )(place, activations)


def own_columns(family_ref, columns):
    shape = (family_ref.shape[0], columns)
    column_family = lax.broadcasted_iota(jnp.int32, shape, 1) // ADAPTER_RANK
    return column_family == family_ref[:, :1].astype(jnp.int32)


def rows_kernel(
    received_ref, up_ref, down_ref, rows_ref, backward_ref, dy, families, up, down, rows, sems
):
    width, columns = down.shape
    features = dy.shape[1]
    steps = width // BLOCK
    first = [
        pltpu.make_async_copy(received_ref.at[:, pl.ds(0, features)], dy, sems.at[0]),
        pltpu.make_async_copy(up_ref, up, sems.at[1]),
        pltpu.make_async_copy(
            received_ref.at[:, pl.ds(features, LANES)], families, sems.at[2]
        ),
    ]
    loads, stores = [], []
    for step in range(steps):
        part = pl.ds(step * BLOCK, BLOCK)
        loads.append(pltpu.make_async_copy(down_ref.at[part], down.at[part], sems.at[3 + step]))
        stores.append(
            pltpu.make_async_copy(
                rows.at[:, part], rows_ref.at[:, part], sems.at[3 + steps + step]
            )
        )
    for copy in first + loads:
        copy.start()
    for copy in first:
        copy.wait()
    back = dot(dy[...], up[...], ((1,), (1,)))
    back = jnp.where(own_columns(families, columns), back, 0.0).astype(jnp.bfloat16)
    backward_ref[...] = back
    for step in range(steps):
        part = pl.ds(step * BLOCK, BLOCK)
        loads[step].wait()
        product = dot(back, down[part], ((1,), (1,)))
        rows[:, part] = (SCALE * product).astype(jnp.bfloat16)
        stores[step].start()
    for copy in stores:
        copy.wait()


def make_rows(received, adapter_up, adapter_down):
    token_slots = received.shape[0]
    columns, features = adapter_up.shape
    width = adapter_down.shape[0]
    return pl.pallas_call(
        rows_kernel,
        in_specs=[pl.BlockSpec(memory_space=pl.ANY)] * 3,
        out_specs=[
            pl.BlockSpec(memory_space=pl.ANY),
            pl.BlockSpec(memory_space=pltpu.VMEM),
        ],
        out_shape=[
            jax.ShapeDtypeStruct((token_slots, width), jnp.bfloat16),
            jax.ShapeDtypeStruct((token_slots, columns), jnp.bfloat16),
        ],
        scratch_shapes=[
            pltpu.VMEM((token_slots, features), jnp.bfloat16),
            pltpu.VMEM((token_slots, LANES), jnp.bfloat16),
            pltpu.VMEM((columns, features), jnp.bfloat16),
            pltpu.VMEM((width, columns), jnp.bfloat16),
            pltpu.VMEM((token_slots, width), jnp.bfloat16),
            pltpu.SemaphoreType.DMA((3 + 2 * (width // BLOCK),)),
        ],
        compiler_params=pltpu.CompilerParams(vmem_limit_bytes=VMEM),
        cost_estimate=pl.CostEstimate(
            flops=2 * token_slots * columns * (width + features),
            bytes_accessed=2 * (columns + token_slots) * (width + features),
            transcendentals=0,
        ),
    )(received, adapter_up, adapter_down)


def grads_kernel(pieces, *refs):
    dy_ref, family_ref, backward_ref, down_ref, grad_down_ref, grad_up_ref, low_ref = refs[pieces:]
    step = pl.program_id(0)
    x = refs[0][...]
    if pieces == 2:
        x = jnp.where(step < pl.num_programs(0) - 1, x, refs[1][...])

    @pl.when(step == 0)
    def _():
        low_ref[...] = jnp.zeros_like(low_ref)

    low_ref[...] += dot(x, down_ref[...], ((1,), (0,)))
    grad_down = dot(x, backward_ref[...], ((0,), (0,)))
    grad_down_ref[...] = (SCALE * grad_down).astype(jnp.bfloat16)

    @pl.when(step == pl.num_programs(0) - 1)
    def _():
        keep = own_columns(family_ref, low_ref.shape[1])
        low = jnp.where(keep, low_ref[...], 0.0).astype(jnp.bfloat16)
        grad_up = dot(low, dy_ref[...], ((0,), (0,)))
        grad_up_ref[...] = (SCALE * grad_up).astype(jnp.bfloat16)


def make_grads(xs, received, backward_rows, adapter_up, adapter_down):
    token_slots = received.shape[0]
    columns, features = adapter_up.shape
    width = adapter_down.shape[0]
    blocks = xs[0].shape[1] // BLOCK
    return pl.pallas_call(
        functools.partial(grads_kernel, len(xs)),
        grid=(width // BLOCK,),
        in_specs=[
            pl.BlockSpec((token_slots, BLOCK), lambda j: (0, jnp.minimum(j, blocks - 1))),
            *[pl.BlockSpec((token_slots, BLOCK), lambda j: (0, 0)) for _ in xs[1:]],
            pl.BlockSpec((token_slots, features), lambda j: (0, 0)),
            pl.BlockSpec((token_slots, LANES), lambda j: (0, features // LANES)),
            pl.BlockSpec((token_slots, columns), lambda j: (0, 0)),
            pl.BlockSpec((BLOCK, columns), lambda j: (j, 0)),
        ],
        out_specs=[
            pl.BlockSpec((BLOCK, columns), lambda j: (j, 0)),
            pl.BlockSpec((columns, features), lambda j: (0, 0)),
        ],
        out_shape=[
            jax.ShapeDtypeStruct((width, columns), jnp.bfloat16),
            jax.ShapeDtypeStruct((columns, features), jnp.bfloat16),
        ],
        scratch_shapes=[pltpu.VMEM((token_slots, columns), jnp.float32)],
        compiler_params=pltpu.CompilerParams(vmem_limit_bytes=VMEM // 2),
        cost_estimate=pl.CostEstimate(
            flops=2 * token_slots * columns * (2 * width + features),
            bytes_accessed=2 * (2 * columns + token_slots) * (width + features),
            transcendentals=0,
        ),
    )(*xs, received, received, backward_rows, adapter_down)


def finish_kernel(
    share, groups, at_ref, place_ref, rows_ref, base, out_ref, rows, out, sems
):
    inner = PLANE // groups
    wide = PLANE * share
    layers = max(1, LANES // share)
    steps = base.shape[2] // (layers * share)
    loads, stores = [], []
    for step in range(steps):
        part = pl.ds(step * layers * wide, layers * wide)
        loads.append(
            pltpu.make_async_copy(rows_ref.at[:, part], rows.at[:, part], sems.at[step])
        )
        stores.append(
            pltpu.make_async_copy(
                out.at[:, part], out_ref.at[:, part], sems.at[steps + step]
            )
        )
    for copy in loads:
        copy.start()
    for step in range(steps):
        loads[step].wait()
        for layer in range(step * layers, (step + 1) * layers):
            for block in range(PLANE):
                columns = pl.ds((layer * PLANE + block) * share, share)
                adapter_part = dot(place_ref[...], rows[:, columns], ((1,), (0,)))
                inner_shift = lax.rem(at_ref[0] - block // groups + inner, inner)
                group_shift = lax.rem(at_ref[1] - block % groups + groups, groups)
                frozen_part = base[inner_shift * groups + group_shift]
                frozen_part = frozen_part[:, layer * share : (layer + 1) * share]
                total = frozen_part.astype(jnp.float32) + adapter_part
                out[:, columns] = total.astype(jnp.bfloat16)
        stores[step].start()
    for copy in stores:
        copy.wait()


def finish(at, place, rows, base, deep, groups):
    tok_rows, token_slots = place.shape
    width = rows.shape[1]
    share = base.shape[2] // deep
    steps = deep // max(1, LANES // share)
    return pl.pallas_call(
        functools.partial(finish_kernel, share, groups),
        in_specs=[
            pl.BlockSpec(memory_space=pltpu.SMEM),
            pl.BlockSpec(memory_space=pltpu.VMEM),
            pl.BlockSpec(memory_space=pl.ANY),
            pl.BlockSpec(memory_space=pltpu.VMEM),
        ],
        out_specs=pl.BlockSpec(memory_space=pl.ANY),
        out_shape=jax.ShapeDtypeStruct((tok_rows, width), jnp.bfloat16),
        scratch_shapes=[
            pltpu.VMEM(rows.shape, jnp.bfloat16),
            pltpu.VMEM((tok_rows, width), jnp.bfloat16),
            pltpu.SemaphoreType.DMA((2 * steps,)),
        ],
        compiler_params=pltpu.CompilerParams(vmem_limit_bytes=VMEM // 2),
        cost_estimate=pl.CostEstimate(
            flops=2 * tok_rows * token_slots * width,
            bytes_accessed=2 * width * (token_slots + 2 * tok_rows),
            transcendentals=0,
        ),
    )(at, place, rows, base)


def pair_kernel(layer_ref, below_ref, above_ref, over_ref, out_ref):
    share = below_ref.shape[0]

    @pl.when(layer_ref[0] < 2)
    def _():
        out_ref[:share] = above_ref[...]
        out_ref[share:] = over_ref[...]

    @pl.when(layer_ref[0] >= 2)
    def _():
        out_ref[:share] = over_ref[...]
        out_ref[share:] = below_ref[...]


def make_pair(layer, below, above, over):
    share, features = below.shape
    whole = pl.BlockSpec(memory_space=pltpu.VMEM)
    return pl.pallas_call(
        pair_kernel,
        in_specs=[pl.BlockSpec(memory_space=pltpu.SMEM), whole, whole, whole],
        out_specs=whole,
        out_shape=jax.ShapeDtypeStruct((2 * share, features), jnp.bfloat16),
        cost_estimate=pl.CostEstimate(
            flops=EARLY_FLOPS, bytes_accessed=10 * share * features, transcendentals=0
        ),
    )(layer[None], below, above, over)


def to_owners_kernel(rows, at_ref, *refs):
    count = len(refs) // 2
    for turn in range(count):
        start = pl.multiple_of(lax.bitwise_xor(at_ref[0], turn) * rows, rows)
        for block in range(count):
            refs[count + turn][block * rows : (block + 1) * rows] = refs[block][
                pl.ds(start, rows)
            ]


def to_owners(at, blocks):
    whole = pl.BlockSpec(memory_space=pltpu.VMEM)
    return pl.pallas_call(
        functools.partial(to_owners_kernel, blocks[0].shape[0] // len(blocks)),
        in_specs=[pl.BlockSpec(memory_space=pltpu.SMEM)] + [whole] * len(blocks),
        out_specs=[whole] * len(blocks),
        out_shape=[jax.ShapeDtypeStruct(b.shape, b.dtype) for b in blocks],
        cost_estimate=pl.CostEstimate(
            flops=EARLY_FLOPS, bytes_accessed=4 * len(blocks) * blocks[0].size, transcendentals=0
        ),
    )(at, *blocks)


def by_sender_kernel(rows, at_ref, *refs):
    count = len(refs) - 1
    for turn in range(count):
        for block in range(count):
            layer = lax.bitwise_xor(at_ref[1], block)
            sender = layer * count + lax.bitwise_xor(at_ref[0], turn)
            start = pl.multiple_of(sender * rows, rows)
            refs[count][pl.ds(start, rows)] = refs[turn][block * rows : (block + 1) * rows]


def by_sender(at, blocks):
    whole = pl.BlockSpec(memory_space=pltpu.VMEM)
    slots, columns = blocks[0].shape
    return pl.pallas_call(
        functools.partial(by_sender_kernel, slots // len(blocks)),
        in_specs=[pl.BlockSpec(memory_space=pltpu.SMEM)] + [whole] * len(blocks),
        out_specs=whole,
        out_shape=jax.ShapeDtypeStruct((slots * len(blocks), columns), jnp.bfloat16),
    )(at, *blocks)


def local(activations, cotangent, family, value_weight, adapter_down, adapter_up):
    count = lax.axis_size("adapter")
    groups = lax.axis_size("groups")
    inner = PLANE // groups
    deep = count // inner
    tok_rows, width = activations.shape
    cap = max(2, (2 * tok_rows + count - 1) // count)
    token_slots = count * cap
    me = lax.axis_index("adapter")
    my_group = lax.axis_index("groups")
    my_inner = lax.rem(me, inner)
    my_layer = me // inner

    def next_layer(block, step):
        pairs = [(j, j + step) for j in range(count) if 0 <= j + step < count]
        return lax.ppermute(block, "adapter", pairs)

    def send_layers(block, layers):
        pairs = [(j * inner + at, k * inner + at) for j, k in layers for at in range(inner)]
        return lax.ppermute(block, "adapter", pairs)

    def turned(block, bits, step):
        pairs = [(j, (j // step ^ bits) * step + j % step) for j in range(count)]
        return lax.ppermute(block, "adapter", pairs)

    def pick(layer, *blocks):
        return lax.select_n(layer, *blocks)

    def around_groups(block, shift):
        pairs = [(j, (j + shift) % groups) for j in range(groups)]
        return lax.ppermute(block, "groups", pairs)

    def around_plane(block, shift):
        pairs = [
            (line * inner + j, line * inner + (j + shift) % inner)
            for line in range(deep)
            for j in range(inner)
        ]
        return lax.ppermute(block, "adapter", pairs)

    share = value_weight.shape[0] // groups
    own_share = lax.dynamic_slice_in_dim(value_weight, my_group * share, share, 0)
    family, own_share = lax.optimization_barrier((family, own_share))
    hops = [next_layer(own_share, inner), next_layer(own_share, -inner)]
    if deep > 4:
        for step in range(2, deep):
            hops += [next_layer(own_share, step * inner), next_layer(own_share, -step * inner)]

    send, place = pack(family, cotangent, cap, token_slots)
    received = lax.all_to_all(send, "adapter", split_axis=0, concat_axis=0, tiled=True)
    split = deep == inner == 4 and width > BLOCK
    send_x = pack_x(place, activations, width - BLOCK if split else None)
    received, own_share, cotangent, send_x = lax.optimization_barrier(
        (received, own_share, cotangent, send_x)
    )
    if deep == 4:
        hops.append(send_layers(own_share, ((0, 2), (3, 1))))
    received_input = lax.all_to_all(send_x, "adapter", split_axis=0, concat_axis=0, tiled=True)

    plane_dy = [cotangent] + [around_groups(cotangent, -shift) for shift in range(1, groups)]
    plane_dy = jnp.stack(plane_dy)
    plane_dy = [plane_dy] + [around_plane(plane_dy, -shift) for shift in range(1, inner)]
    adapter_rows, backward_rows = make_rows(received, adapter_up, adapter_down)

    if deep == 4:
        hops.append(send_layers(make_pair(my_layer, *hops), ((1, 0), (2, 3))))
    crossed = []
    if split:
        last = dot(place, activations[:, width - BLOCK :], ((1,), (0,))).astype(jnp.bfloat16)
        last, backward_rows = lax.optimization_barrier((last, backward_rows))
        slots = token_slots // deep
        for k in range(deep):
            start = lax.bitwise_xor(my_layer, jnp.int32(k)) * slots
            block = lax.dynamic_slice_in_dim(last, start, slots, 0)
            crossed.append(turned(block, k, inner) if k else block)
    received_input, adapter_rows, plane_dy, hops = lax.optimization_barrier(
        (received_input, adapter_rows, plane_dy, hops)
    )
    returned_rows = lax.all_to_all(adapter_rows, "adapter", split_axis=0, concat_axis=0, tiled=True)
    if deep == 4:
        below, above, over, pair = hops
        first, second = pair[:share], pair[share:]
        plane_weight = jnp.concatenate(
            [
                pick(my_layer, own_share, below, over, first),
                pick(my_layer, above, own_share, below, second),
                pick(my_layer, first, above, own_share, below),
                pick(my_layer, second, over, above, own_share),
            ],
            axis=0,
        )
    else:
        plane_weight = lax.dynamic_slice_in_dim(
            jnp.concatenate(hops[0::2][::-1] + [own_share] + hops[1::2], axis=0),
            (deep - 1 - my_layer) * share,
            deep * share,
            0,
        )
    plane_dy = [jnp.concatenate([d[s] for d in plane_dy], axis=0) for s in range(groups)]

    blocks = [dot(block, plane_weight, ((1,), (1,))).astype(jnp.bfloat16) for block in plane_dy]
    blocks = blocks[:1] + [around_groups(block, s) for s, block in enumerate(blocks) if s]
    at = jnp.stack([my_inner, my_layer]).astype(jnp.int32)
    xs = [received_input]
    if split:
        crossed = to_owners(at, crossed)
        crossed = [turned(block, k, 1) if k else block for k, block in enumerate(crossed)]
        xs.append(by_sender(at, crossed))
    base = []
    for shift in range(inner):
        for block in blocks:
            piece = block[shift * tok_rows : (shift + 1) * tok_rows]
            base.append(around_plane(piece, shift) if shift else piece)
    base = jnp.stack(base)
    xs, base = lax.optimization_barrier((xs, base))
    grad_down, grad_up = make_grads(
        xs, received, backward_rows, adapter_up, adapter_down
    )
    at = jnp.stack([my_inner, my_group]).astype(jnp.int32)
    input_gradient = finish(at, place.T, returned_rows, base, deep, groups)
    return (input_gradient, grad_down, grad_up)


def solution(mesh):
    in_specs = (
        P(("groups", "adapter"), None),
        P(("groups", "adapter"), None),
        P(("groups", "adapter")),
        P("adapter", None),
        P(None, "adapter"),
        P("adapter", None),
    )
    out_specs = (P(("groups", "adapter"), None), P("groups", "adapter"), P("adapter", "groups"))
    return jax.shard_map(local, mesh=mesh, in_specs=in_specs, out_specs=out_specs, check_vma=False)
```
